32 devices in a mesh: dp: 8 (over z, x), tensor: 4 (over y, core).
Axes of the slice: x: 2, y: 2, z: 4, core: 2. Of those that a mesh axis runs over, the one named last changes fastest.
Arguments:
- hidden_states: bfloat16 [1024, 6144], P('dp', 'tensor'), may hold values from -9 to 9
- expert_ids: int32 [1024, 2], P('dp'), may hold values from 0 to 7, as said below
- route_gates: float32 [1024, 2], P('dp'), may hold values from 0.1 to 0.9
- gate_weight: bfloat16 [6144, 16384], P('tensor', 'dp'), may hold values from -0.078125 to 0.078125
- up_weight: bfloat16 [6144, 16384], P('tensor', 'dp'), may hold values from -0.078125 to 0.078125
Outputs:
- covariance: float32 [16384, 16384], P('tensor', 'dp')
The draws below stay inside these ranges and needn't reach their ends.
Inputs may be any that keep to these rules, and one draw needn't show every extreme that they name: `expert_ids`: each row names two different experts. Among the 128 rows of one device (aligned blocks), expert 0 is named by at most 32 rows, by exactly 32 rows in at least one block, and by at least one row in every block.
All inputs are finite; a program needn't handle non-finite values.
Results may differ from the reference program's by a relative error of at most 0.0057.
Values may be sent and summed in bfloat16 or wider, within the bound.
No kernel may reach another device: no remote copies, remote signals or barrier semaphores. Data moves between devices by JAX's collectives and lax.ppermute only.
A program may use at most 128 MiB of HBM per device.

```python
import jax
import jax.numpy as jnp

D = 6144
FF = 16384
EXPERTS = 8
TOK_DEV = 128
CAP = 32
TOKENS = 1024
N_DP = 8


def draw_expert_ids(key, part):
    blocks = TOKENS // TOK_DEV
    subkeys = jax.random.split(key, 6)
    counts = jax.random.randint(subkeys[0], (blocks,), max(1, CAP // 4), CAP + 1)
    busiest = jax.random.randint(subkeys[1], (), 0, blocks)
    counts = jnp.where(jnp.arange(blocks) == busiest, CAP, counts)
    ranking = jax.vmap(lambda subkey: jax.random.permutation(subkey, TOK_DEV))(jax.random.split(subkeys[2], blocks))
    member = ranking < counts[:, None]
    first_other = jax.random.randint(subkeys[3], (blocks, TOK_DEV), 1, EXPERTS)
    offset = jax.random.randint(subkeys[4], (blocks, TOK_DEV), 1, EXPERTS - 1)
    second_other = 1 + (first_other - 1 + offset) % (EXPERTS - 1)
    first_pick = jnp.where(member, 0, first_other)
    second_pick = jnp.where(member, first_other, second_other)
    flipped = jax.random.randint(subkeys[5], (blocks, TOK_DEV), 0, 2) == 1
    left_pick = jnp.where(flipped, second_pick, first_pick)
    right_pick = jnp.where(flipped, first_pick, second_pick)
    return jnp.stack([left_pick, right_pick], axis=-1).reshape(TOKENS, 2).astype(jnp.int32)


def level_of(key, dims, pieces, smallest, high):
    loudness = 1.0
    for axis_at, parts in pieces:
        heights = jax.random.uniform(jax.random.fold_in(jax.random.fold_in(key, 6), axis_at), (parts,), jnp.float32, smallest / len(pieces), high / len(pieces))
        loudness = loudness * jnp.repeat(jnp.exp(heights), dims[axis_at] // parts).reshape((-1,) + (1,) * (len(dims) - 1 - axis_at))
    return loudness


def gaussian(key, dims, width, reach, shards=(), kind=jnp.bfloat16):
    result = jax.random.normal(key, dims, jnp.float32) * width
    if len(shards) > 0:
        result = level_of(key, dims, shards, -0.22, 0.18) * result
    return jnp.clip(result, min=-reach, max=reach).astype(kind)


def setup_inputs(seed: int = 0) -> dict:
    key_of = jax.random.split(jax.random.key(seed), 6)
    hidden_states = gaussian(key_of[0], (TOKENS, D), 1.5, 9.0, ((0, 8), (1, 4)))
    expert_ids = draw_expert_ids(jax.random.fold_in(key_of[5], 71), 0)
    route_gates = jnp.clip(0.1 + 0.79999997 * jax.random.uniform(key_of[2], (TOKENS, 2), jnp.float32) ** level_of(key_of[2], (TOKENS, 2), ((0, 8),), -0.2, 0.2), 0.1, 0.9)
    gate_weight = gaussian(key_of[3], (D, FF), D ** -0.5, 0.078125, ((0, 4), (1, 8)))
    up_weight = gaussian(key_of[4], (D, FF), D ** -0.5, 0.078125, ((0, 4), (1, 8)))
    return dict(hidden_states=hidden_states, expert_ids=expert_ids, route_gates=route_gates, gate_weight=gate_weight, up_weight=up_weight)


def pack_rows(token_blocks, weight_blocks):
    member = (weight_blocks > 0).astype(jnp.int32)
    position = jnp.cumsum(member, axis=1) - 1
    slot_index = jnp.arange(CAP, dtype=jnp.int32)
    picked = (position[:, None, :] == slot_index[None, :, None]) & (member[:, None, :] > 0)
    selector = picked.astype(jnp.float32)
    packed = jnp.einsum("sct,std->scd", selector, token_blocks.astype(jnp.float32)).astype(jnp.bfloat16)
    packed_weight = jnp.einsum("sct,st->sc", selector, weight_blocks.astype(jnp.float32)).astype(jnp.bfloat16)
    return packed.reshape(-1, token_blocks.shape[2]), packed_weight.reshape(-1)


def reference(hidden_states, expert_ids, route_gates, gate_weight, up_weight):
    route_weight = jnp.sum(jnp.where(expert_ids == 0, route_gates, jnp.zeros_like(route_gates)), axis=1).astype(jnp.bfloat16)
    packed_rows, packed_weight = pack_rows(hidden_states.reshape(N_DP, TOK_DEV, D), route_weight.reshape(N_DP, TOK_DEV))
    weight_total = jnp.sum(packed_weight.astype(jnp.float32))
    pre_gate = jnp.dot(packed_rows, gate_weight, preferred_element_type=jnp.float32)
    pre_up = jnp.dot(packed_rows, up_weight, preferred_element_type=jnp.float32)
    key_rows = (jax.nn.silu(pre_gate) * pre_up).astype(jnp.bfloat16)
    weighted = (packed_weight.astype(jnp.float32)[:, None] * key_rows.astype(jnp.float32)).astype(jnp.bfloat16)
    covariance = jnp.dot(key_rows.T, weighted, preferred_element_type=jnp.float32)
    return covariance / weight_total
```

```python
import jax
import jax.numpy as jnp
from jax import lax
from jax.experimental import pallas as pl
from jax.experimental.pallas import tpu as pltpu
from jax.sharding import PartitionSpec as P

CAP = 32
LANES = 128
BF, F32 = jnp.bfloat16, jnp.float32
AXES = ("dp", "tensor")
ROWS_OF = (((0,), (0,)), ((), ()))


def pack_rows(token_blocks, weight_blocks):
    member = (weight_blocks > 0).astype(jnp.int32)
    position = jnp.cumsum(member, axis=1) - 1
    slot_index = lax.broadcasted_iota(jnp.int32, (1, CAP, 1), 1)
    picked = (position[:, None, :] == slot_index) & (member[:, None, :] > 0)
    selector = picked.astype(BF)
    packed = jnp.einsum(
        "sct,std->scd", selector, token_blocks, preferred_element_type=F32
    ).astype(BF)
    packed_weight = jnp.einsum(
        "sct,st->sc", selector, weight_blocks, preferred_element_type=F32
    ).astype(BF)
    return (packed.reshape(-1, token_blocks.shape[2]), packed_weight.reshape(-1))


def any_mesh(hidden_states, expert_ids, route_gates, gate_weight, up_weight):
    route_weight = jnp.sum(
        jnp.where(expert_ids == 0, route_gates, jnp.zeros_like(route_gates)), axis=1
    ).astype(BF)
    own_rows, own_weight = pack_rows(hidden_states[None], route_weight[None])
    packed_rows, packed_weight = (
        lax.all_gather(own_rows, "dp", axis=0, tiled=True),
        lax.all_gather(own_weight, "dp", axis=0, tiled=True),
    )
    weight_total = jnp.sum(packed_weight.astype(F32))
    gate_part = jnp.dot(packed_rows, gate_weight, preferred_element_type=F32)
    up_part = jnp.dot(packed_rows, up_weight, preferred_element_type=F32)
    summed = lax.psum_scatter(
        jnp.concatenate([gate_part, up_part], axis=1), "tensor", scatter_dimension=0, tiled=True
    )
    unit_width = gate_weight.shape[1]
    local_keys = (jax.nn.silu(summed[:, :unit_width]) * summed[:, unit_width:]).astype(BF)
    column_keys = lax.all_gather(local_keys, "tensor", axis=0, tiled=True)
    weighted = (packed_weight.astype(F32)[:, None] * column_keys.astype(F32)).astype(BF)
    spread_keys = lax.all_gather(local_keys, "dp", axis=1, tiled=True)
    row_keys = lax.all_to_all(spread_keys, "tensor", split_axis=1, concat_axis=0, tiled=True)
    covariance = lax.dot_general(row_keys, weighted, ROWS_OF, preferred_element_type=F32)
    return covariance / weight_total


def pairs(to):
    number = lambda z, x, y, c: z * 8 + x * 4 + y * 2 + c
    out = []
    for z in range(4):
        for x in range(2):
            for y in range(2):
                for c in range(2):
                    there = to(z, x, y, c)
                    if there is not None:
                        out.append((number(z, x, y, c), number(*there)))
    return out


CORE = pairs(lambda z, x, y, c: (z, x, y, 1 - c))
Y = pairs(lambda z, x, y, c: (z, x, 1 - y, c))
X = pairs(lambda z, x, y, c: (z, 1 - x, y, c))
Z1 = pairs(lambda z, x, y, c: (z ^ 1, x, y, c))
Z2 = pairs(lambda z, x, y, c: (z ^ 2, x, y, c))
XZ1 = pairs(lambda z, x, y, c: (z ^ 1, 1 - x, y, c))
HOME_Z2 = pairs(lambda z, x, y, c: (z ^ 2, x, y, c) if c == z % 2 else None)
HOME_Y = pairs(lambda z, x, y, c: (z, x, 1 - y, c) if c == z % 2 and y == z // 2 else None)
HOME_Z1 = pairs(lambda z, x, y, c: (z ^ 1, x, y, c) if c == z % 2 else None)


def send(value, route):
    return lax.ppermute(value, AXES, route)


def pack_kernel(ids_ref, gates_ref, tokens_ref, out_ref):
    tokens, width = tokens_ref.shape
    weight = jnp.sum(
        jnp.where(ids_ref[...] == 0, gates_ref[...], 0.0), axis=1, keepdims=True
    ).astype(BF)
    member = weight.astype(F32) > 0
    earlier = lax.broadcasted_iota(jnp.int32, (tokens, tokens), 1) <= lax.broadcasted_iota(
        jnp.int32, (tokens, tokens), 0
    )
    spread = jnp.broadcast_to(member.astype(F32), (tokens, LANES)).astype(BF)
    position = jnp.dot(earlier.astype(BF), spread, preferred_element_type=F32) - 1.0
    slot = lax.broadcasted_iota(jnp.int32, (tokens, CAP), 1).astype(F32)
    picked = jnp.where((position[:, :CAP] == slot) & member, 1.0, 0.0).astype(BF)
    out_ref[:, :width] = lax.dot_general(
        picked, tokens_ref[...], ROWS_OF, preferred_element_type=F32
    ).astype(BF)
    weights = jnp.broadcast_to(weight, (tokens, LANES))
    out_ref[:, width:] = lax.dot_general(
        picked, weights, ROWS_OF, preferred_element_type=F32
    ).astype(BF)


def pack(hidden_states, expert_ids, route_gates):
    return pl.pallas_call(
        pack_kernel,
        out_shape=jax.ShapeDtypeStruct((CAP, hidden_states.shape[1] + LANES), BF),
    )(expert_ids, route_gates, hidden_states)


def half(flag, value, width):
    return jnp.where(flag == 0, value[..., :width], value[..., width:])


def fast(hidden_states, expert_ids, route_gates, gate_weight, up_weight):
    depth, units = gate_weight.shape
    dp, tensor = lax.axis_index("dp"), lax.axis_index("tensor")
    z, x, y, core = dp // 2, dp % 2, tensor // 2, tensor % 2
    home, inside = core == z % 2, y == z // 2

    own = pack(hidden_states, expert_ids, route_gates)
    far = send(own, Z2)
    place = (z % 2) * 2 + x

    def chunk(mine):
        beside = {1: send(mine, X), 2: send(mine, Z1), 3: send(mine, XZ1)}
        beside[0] = mine
        rows = []
        for at in range(4):
            differs = place ^ at
            block = beside[0]
            for k in (1, 2, 3):
                block = jnp.where(differs == k, beside[k], block)
            rows.append(block)
        return jnp.concatenate(rows, axis=0)

    def keys_of(tokens):
        rows = tokens[:, :depth]
        parts = jnp.stack(
            [
                jnp.dot(rows, gate_weight, preferred_element_type=F32),
                jnp.dot(rows, up_weight, preferred_element_type=F32),
            ]
        )
        quarter = units // 4
        parts = parts.reshape(2, rows.shape[0], 4, quarter)
        kept = jnp.where(core == 0, parts[:, :, 0::2], parts[:, :, 1::2])
        given = jnp.where(core == 0, parts[:, :, 1::2], parts[:, :, 0::2]).astype(BF)
        summed = kept + send(given, CORE).astype(F32)
        kept = jnp.where(y == 0, summed[:, :, 0], summed[:, :, 1])
        given = jnp.where(y == 0, summed[:, :, 1], summed[:, :, 0]).astype(BF)
        total = kept + send(given, Y).astype(F32)
        return (jax.nn.silu(total[0]) * total[1]).astype(BF)

    def spread(quarter):
        across = send(quarter, Y)
        both = jnp.stack([quarter, across])
        other = send(both, CORE)
        low, high = jnp.where(core == 0, both, other), jnp.where(core == 0, other, both)
        halves = jnp.concatenate([low, high], axis=2)
        mine, others = halves[0], halves[1]
        got = send(mine, HOME_Z2)
        got_across = send(got, HOME_Y)
        mine_s = jnp.where(inside, mine, got)
        others_s = jnp.where(inside, others, got_across)
        own_slice = jnp.concatenate(
            [jnp.where(y == 0, mine, others), jnp.where(y == 0, others, mine)], axis=1
        )
        panel = jnp.concatenate(
            [jnp.where(y == 0, mine_s, others_s), jnp.where(y == 0, others_s, mine_s)], axis=1
        )
        panel = jnp.where(home, panel, send(panel, HOME_Z1))
        return own_slice, panel, send(panel, X)

    tokens = [chunk(own), chunk(far)]
    weights = [each[:, depth : depth + 1].astype(F32) for each in tokens]
    weight_total = jnp.sum(weights[0]) + jnp.sum(weights[1])
    parts = [spread(keys_of(each)) for each in tokens]
    weighted = [(w * p[0].astype(F32)).astype(BF) for w, p in zip(weights, parts)]
    columns = jnp.concatenate(
        [
            jnp.where(inside, weighted[0], weighted[1]),
            jnp.where(inside, weighted[1], weighted[0]),
        ]
    )
    panel_own = jnp.concatenate([p[1] for p in parts])
    panel_other = jnp.concatenate([p[2] for p in parts])
    panel = jnp.concatenate(
        [jnp.where(x == 0, panel_own, panel_other), jnp.where(x == 0, panel_other, panel_own)],
        axis=1,
    )
    covariance = lax.dot_general(panel, columns, ROWS_OF, preferred_element_type=F32)
    return covariance / weight_total


def solution(mesh):
    placed = (P("dp", "tensor"), P("dp", None), P("dp", None), P("tensor", "dp"), P("tensor", "dp"))
    sizes = (mesh.shape["dp"], mesh.shape["tensor"])
    return jax.shard_map(
        fast if sizes == (8, 4) else any_mesh,
        mesh=mesh,
        in_specs=placed,
        out_specs=P("tensor", "dp"),
        check_vma=False,
    )
```

```python
import jax
import jax.numpy as jnp
from jax import lax
from jax.experimental import pallas as pl
from jax.experimental.pallas import tpu as pltpu
from jax.sharding import PartitionSpec as P

CAP = 32
LANES = 128
BF, F32 = jnp.bfloat16, jnp.float32
AXES = ("dp", "tensor")
ROWS_OF = (((0,), (0,)), ((), ()))


def pack_rows(token_blocks, weight_blocks):
    member = (weight_blocks > 0).astype(jnp.int32)
    position = jnp.cumsum(member, axis=1) - 1
    slot_index = lax.broadcasted_iota(jnp.int32, (1, CAP, 1), 1)
    picked = (position[:, None, :] == slot_index) & (member[:, None, :] > 0)
    selector = picked.astype(BF)
    packed = jnp.einsum(
        "sct,std->scd", selector, token_blocks, preferred_element_type=F32
    ).astype(BF)
    packed_weight = jnp.einsum(
        "sct,st->sc", selector, weight_blocks, preferred_element_type=F32
    ).astype(BF)
    return (packed.reshape(-1, token_blocks.shape[2]), packed_weight.reshape(-1))


def any_mesh(hidden_states, expert_ids, route_gates, gate_weight, up_weight):
    route_weight = jnp.sum(
        jnp.where(expert_ids == 0, route_gates, jnp.zeros_like(route_gates)), axis=1
    ).astype(BF)
    own_rows, own_weight = pack_rows(hidden_states[None], route_weight[None])
    packed_rows, packed_weight = (
        lax.all_gather(own_rows, "dp", axis=0, tiled=True),
        lax.all_gather(own_weight, "dp", axis=0, tiled=True),
    )
    weight_total = jnp.sum(packed_weight.astype(F32))
    gate_part = jnp.dot(packed_rows, gate_weight, preferred_element_type=F32)
    up_part = jnp.dot(packed_rows, up_weight, preferred_element_type=F32)
    summed = lax.psum_scatter(
        jnp.concatenate([gate_part, up_part], axis=1), "tensor", scatter_dimension=0, tiled=True
    )
    unit_width = gate_weight.shape[1]
    local_keys = (jax.nn.silu(summed[:, :unit_width]) * summed[:, unit_width:]).astype(BF)
    column_keys = lax.all_gather(local_keys, "tensor", axis=0, tiled=True)
    weighted = (packed_weight.astype(F32)[:, None] * column_keys.astype(F32)).astype(BF)
    spread_keys = lax.all_gather(local_keys, "dp", axis=1, tiled=True)
    row_keys = lax.all_to_all(spread_keys, "tensor", split_axis=1, concat_axis=0, tiled=True)
    covariance = lax.dot_general(row_keys, weighted, ROWS_OF, preferred_element_type=F32)
    return covariance / weight_total


def pairs(to):
    number = lambda z, x, y, c: z * 8 + x * 4 + y * 2 + c
    out = []
    for z in range(4):
        for x in range(2):
            for y in range(2):
                for c in range(2):
                    there = to(z, x, y, c)
                    if there is not None:
                        out.append((number(z, x, y, c), number(*there)))
    return out


def inside(z, y):
    return z // 2 == y


CORE = pairs(lambda z, x, y, c: (z, x, y, 1 - c))
Y = pairs(lambda z, x, y, c: (z, x, 1 - y, c))
X = pairs(lambda z, x, y, c: (z, 1 - x, y, c))
Z1 = pairs(lambda z, x, y, c: (z ^ 1, x, y, c))
Z2 = pairs(lambda z, x, y, c: (z ^ 2, x, y, c))
XZ1 = pairs(lambda z, x, y, c: (z ^ 1, 1 - x, y, c))
FAR = pairs(lambda z, x, y, c: (z ^ 2, x, y, c) if inside(z, y) else None)
FAR_Y = pairs(lambda z, x, y, c: (z ^ 2, x, 1 - y, c) if not inside(z, y) else None)
HOME_X = pairs(lambda z, x, y, c: (z, 1 - x, y, c) if c == z % 2 else None)
HOME_Z1 = pairs(lambda z, x, y, c: (z ^ 1, x, y, c) if c == z % 2 else None)
AWAY_X = pairs(lambda z, x, y, c: (z, 1 - x, y, c) if c != z % 2 else None)


def send(value, route):
    return lax.ppermute(value, AXES, route)


def pack_kernel(ids_ref, gates_ref, tokens_ref, out_ref):
    tokens, width = tokens_ref.shape
    weight = jnp.sum(jnp.where(ids_ref[...] == 0, gates_ref[...], 0.0), axis=0, keepdims=True)
    weight = weight.astype(BF).astype(F32)
    member = jnp.where(weight > 0, 1.0, 0.0)
    earlier = lax.broadcasted_iota(jnp.int32, (tokens, tokens), 0) <= lax.broadcasted_iota(
        jnp.int32, (tokens, tokens), 1
    )
    position = jnp.dot(
        jnp.broadcast_to(member, (8, tokens)).astype(BF),
        jnp.where(earlier, 1.0, 0.0).astype(BF),
        preferred_element_type=F32,
    )[:1]
    slot = lax.broadcasted_iota(jnp.int32, (CAP, tokens), 0).astype(F32)
    picked = jnp.where((position - 1.0 == slot) & (member > 0), 1.0, 0.0)
    out_ref[:, :width] = jnp.dot(
        picked.astype(BF), tokens_ref[...], preferred_element_type=F32
    ).astype(BF)
    weights = jnp.sum(picked * weight, axis=1, keepdims=True)
    out_ref[:, width:] = jnp.broadcast_to(weights, (CAP, LANES)).astype(BF)


def pack(hidden_states, expert_ids, route_gates):
    return pl.pallas_call(
        pack_kernel,
        out_shape=jax.ShapeDtypeStruct((CAP, hidden_states.shape[1] + LANES), BF),
    )(expert_ids.T, route_gates.T, hidden_states)


TILE = 256


def project_kernel(at_ref, *refs):
    blocks, (gate_ref, up_ref, out_ref, rows_ref) = refs[:4], refs[4:]
    depth, width = gate_ref.shape
    inner = pl.program_id(1)

    @pl.when((pl.program_id(0) == 0) & (inner == 0))
    def _():
        for k, block in enumerate(blocks):
            start = pl.multiple_of((at_ref[0] ^ k) * CAP, CAP)
            rows_ref[pl.ds(start, CAP), :] = block[:, :depth]

    rows = rows_ref[...]
    half = out_ref.shape[2] // 2
    here = pl.multiple_of(inner * width, LANES)
    there = pl.multiple_of(half + inner * width, LANES)
    out_ref[0, :, pl.ds(here, width)] = jnp.dot(rows, gate_ref[...], preferred_element_type=F32)
    out_ref[0, :, pl.ds(there, width)] = jnp.dot(rows, up_ref[...], preferred_element_type=F32)


def project(at, blocks, gate_weight, up_weight):
    depth, units = gate_weight.shape
    quarter = units // 4
    tiles = quarter // TILE
    rows = 4 * CAP
    weight_spec = pl.BlockSpec((depth, TILE), lambda i, j, at: (0, at[1 + i] * tiles + j))
    return pl.pallas_call(
        project_kernel,
        grid_spec=pltpu.PrefetchScalarGridSpec(
            num_scalar_prefetch=1,
            grid=(2, tiles),
            in_specs=[pl.BlockSpec(b.shape, lambda i, j, at: (0, 0)) for b in blocks]
            + [weight_spec, weight_spec],
            out_specs=pl.BlockSpec((1, rows, 2 * quarter), lambda i, j, at: (i, 0, 0)),
            scratch_shapes=[pltpu.VMEM((rows, depth), BF)],
        ),
        out_shape=jax.ShapeDtypeStruct((2, rows, 2 * quarter), F32),
        cost_estimate=pl.CostEstimate(
            flops=2 * rows * depth * units, bytes_accessed=2 * depth * units, transcendentals=0
        ),
    )(at, *blocks, gate_weight, up_weight)


def covariance_kernel(at_ref, scale_ref, first_ref, second_ref, columns_ref, *refs):
    out_ref = refs[-1]
    panel = jnp.concatenate([first_ref[...], second_ref[...]], axis=0)
    out_ref[...] = (
        lax.dot_general(panel, columns_ref[...], ROWS_OF, preferred_element_type=F32)
        * scale_ref[0]
    )


PANEL_TILE = 256


def covariance_part(at, scale, panel, columns, out_rows, into):
    rows, units = panel[0].shape
    steps = units // PANEL_TILE
    panel_spec = pl.BlockSpec((rows, PANEL_TILE), lambda i, at: (0, i))
    in_specs = [
        pl.BlockSpec(memory_space=pltpu.SMEM),
        panel_spec,
        panel_spec,
        pl.BlockSpec(columns.shape, lambda i, at: (0, 0)),
    ]
    args = [at, scale, panel[0], panel[1], columns]
    aliases = {}
    if into is not None:
        in_specs.append(pl.BlockSpec(memory_space=pl.ANY))
        args.append(into)
        aliases = {5: 0}
    width = columns.shape[1]
    return pl.pallas_call(
        covariance_kernel,
        grid_spec=pltpu.PrefetchScalarGridSpec(
            num_scalar_prefetch=1,
            grid=(steps,),
            in_specs=in_specs,
            out_specs=pl.BlockSpec((PANEL_TILE, width), lambda i, at: (at[0] * steps + i, 0)),
        ),
        out_shape=jax.ShapeDtypeStruct((out_rows, width), F32),
        input_output_aliases=aliases,
        cost_estimate=pl.CostEstimate(
            flops=4 * rows * units * width, bytes_accessed=4 * units * width, transcendentals=0
        ),
    )(*args)


def fast(hidden_states, expert_ids, route_gates, gate_weight, up_weight):
    depth, units = gate_weight.shape
    quarter = units // 4
    dp, tensor = lax.axis_index("dp"), lax.axis_index("tensor")
    z, x, y, core = dp // 2, dp % 2, tensor // 2, tensor % 2
    is_home, is_inside = core == z % 2, y == z // 2
    place = (z % 2) * 2 + x
    given_at = jnp.stack([place, (1 - y) * 2 + 1 - core, y * 2 + 1 - core]).astype(jnp.int32)
    kept_at = jnp.stack([place, (1 - y) * 2 + core, y * 2 + core]).astype(jnp.int32)

    def beside(mine):
        return [mine, send(mine, X), send(mine, Z1), send(mine, XZ1)]

    def in_place(blocks):
        rows = []
        for at in range(4):
            block = blocks[0]
            for k in (1, 2, 3):
                block = jnp.where(place ^ at == k, blocks[k], block)
            rows.append(block)
        return jnp.concatenate(rows, axis=0)

    def keys_of(blocks):
        given = project(given_at, blocks, gate_weight, up_weight)
        got = send(given, CORE)
        kept = project(kept_at, blocks, gate_weight, up_weight)
        across = send((kept[0] + got[0]).astype(BF), Y)
        total = kept[1] + got[1] + across.astype(F32)
        return (jax.nn.silu(total[:, :quarter]) * total[:, quarter:]).astype(BF)

    def slice_of(own, other):
        low, high = jnp.where(core == 0, own, other), jnp.where(core == 0, other, own)
        pair = jnp.concatenate([low, high], axis=2)
        return jnp.concatenate(
            [jnp.where(y == 0, pair[0], pair[1]), jnp.where(y == 0, pair[1], pair[0])], axis=1
        )

    def spread(keys):
        far = jnp.stack([send(keys, FAR), send(keys, FAR_Y)])
        near = jnp.stack([keys, send(keys, Y)])
        own_slice = slice_of(near, send(near, CORE))
        far_slice = slice_of(far, send(far, CORE))
        panel = jnp.where(is_inside, own_slice, far_slice)
        along_z, along_x = send(panel, HOME_Z1), send(panel, HOME_X)
        first = jnp.where(is_home, panel, along_z)
        left = send(along_z[:, : units // 2], AWAY_X)
        right = send(along_x[:, units // 2 :], HOME_Z1)
        second = jnp.where(is_home, along_x, jnp.concatenate([left, right], axis=1))
        return own_slice, first, second

    own = pack(hidden_states, expert_ids, route_gates)
    blocks = [beside(own), beside(send(own, Z2))]
    weights = [
        in_place([b[:, depth:] for b in each])[:, :1].astype(F32) for each in blocks
    ]
    scale = (1.0 / (jnp.sum(weights[0]) + jnp.sum(weights[1]))).reshape(1)
    parts = [spread(keys_of(each)) for each in blocks]
    weighted = [(w * p[0].astype(F32)).astype(BF) for w, p in zip(weights, parts)]
    columns = jnp.concatenate(
        [
            jnp.where(is_inside, weighted[0], weighted[1]),
            jnp.where(is_inside, weighted[1], weighted[0]),
        ]
    )
    out_rows = 2 * units
    half_at = jnp.stack([x]).astype(jnp.int32)
    out = covariance_part(half_at, scale, [p[1] for p in parts], columns, out_rows, None)
    return covariance_part(1 - half_at, scale, [p[2] for p in parts], columns, out_rows, out)


def solution(mesh):
    placed = (P("dp", "tensor"), P("dp", None), P("dp", None), P("tensor", "dp"), P("tensor", "dp"))
    sizes = (mesh.shape["dp"], mesh.shape["tensor"])
    return jax.shard_map(
        fast if sizes == (8, 4) else any_mesh,
        mesh=mesh,
        in_specs=placed,
        out_specs=P("tensor", "dp"),
        check_vma=False,
    )
```

```python
import functools

import jax
import jax.numpy as jnp
from jax import lax
from jax.experimental import pallas as pl
from jax.experimental.pallas import tpu as pltpu
from jax.sharding import PartitionSpec as P

CAP = 32
LANES = 128
BF, F32 = jnp.bfloat16, jnp.float32
AXES = ("dp", "tensor")
ROWS_OF = (((0,), (0,)), ((), ()))


def pack_rows(token_blocks, weight_blocks):
    member = (weight_blocks > 0).astype(jnp.int32)
    position = jnp.cumsum(member, axis=1) - 1
    slot_index = lax.broadcasted_iota(jnp.int32, (1, CAP, 1), 1)
    picked = (position[:, None, :] == slot_index) & (member[:, None, :] > 0)
    selector = picked.astype(BF)
    packed = jnp.einsum(
        "sct,std->scd", selector, token_blocks, preferred_element_type=F32
    ).astype(BF)
    packed_weight = jnp.einsum(
        "sct,st->sc", selector, weight_blocks, preferred_element_type=F32
    ).astype(BF)
    return (packed.reshape(-1, token_blocks.shape[2]), packed_weight.reshape(-1))


def any_mesh(hidden_states, expert_ids, route_gates, gate_weight, up_weight):
    route_weight = jnp.sum(
        jnp.where(expert_ids == 0, route_gates, jnp.zeros_like(route_gates)), axis=1
    ).astype(BF)
    own_rows, own_weight = pack_rows(hidden_states[None], route_weight[None])
    packed_rows, packed_weight = (
        lax.all_gather(own_rows, "dp", axis=0, tiled=True),
        lax.all_gather(own_weight, "dp", axis=0, tiled=True),
    )
    weight_total = jnp.sum(packed_weight.astype(F32))
    gate_part = jnp.dot(packed_rows, gate_weight, preferred_element_type=F32)
    up_part = jnp.dot(packed_rows, up_weight, preferred_element_type=F32)
    summed = lax.psum_scatter(
        jnp.concatenate([gate_part, up_part], axis=1), "tensor", scatter_dimension=0, tiled=True
    )
    unit_width = gate_weight.shape[1]
    local_keys = (jax.nn.silu(summed[:, :unit_width]) * summed[:, unit_width:]).astype(BF)
    column_keys = lax.all_gather(local_keys, "tensor", axis=0, tiled=True)
    weighted = (packed_weight.astype(F32)[:, None] * column_keys.astype(F32)).astype(BF)
    spread_keys = lax.all_gather(local_keys, "dp", axis=1, tiled=True)
    row_keys = lax.all_to_all(spread_keys, "tensor", split_axis=1, concat_axis=0, tiled=True)
    covariance = lax.dot_general(row_keys, weighted, ROWS_OF, preferred_element_type=F32)
    return covariance / weight_total


def pairs(to):
    number = lambda z, x, y, c: z * 8 + x * 4 + y * 2 + c
    out = []
    for z in range(4):
        for x in range(2):
            for y in range(2):
                for c in range(2):
                    there = to(z, x, y, c)
                    if there is not None:
                        out.append((number(z, x, y, c), number(*there)))
    return out


def inside(z, y):
    return z // 2 == y


CORE = pairs(lambda z, x, y, c: (z, x, y, 1 - c))
Y = pairs(lambda z, x, y, c: (z, x, 1 - y, c))
X = pairs(lambda z, x, y, c: (z, 1 - x, y, c))
Z1 = pairs(lambda z, x, y, c: (z ^ 1, x, y, c))
Z2 = pairs(lambda z, x, y, c: (z ^ 2, x, y, c))
XZ1 = pairs(lambda z, x, y, c: (z ^ 1, 1 - x, y, c))
FAR = pairs(lambda z, x, y, c: (z ^ 2, x, y, c) if inside(z, y) else None)
FAR_Y = pairs(lambda z, x, y, c: (z ^ 2, x, 1 - y, c) if not inside(z, y) else None)
SHARE = pairs(lambda z, x, y, c: (z ^ 1, x, y, c) if c == z % 2 else (z, 1 - x, y, 1 - c))
HOME_Z1 = pairs(lambda z, x, y, c: (z ^ 1, x, y, c) if c == z % 2 else None)
AWAY_X = pairs(lambda z, x, y, c: (z, 1 - x, y, c) if c != z % 2 else None)

VM = pl.BlockSpec(memory_space=pltpu.VMEM)
SM = pl.BlockSpec(memory_space=pltpu.SMEM)


def send(value, route):
    return lax.ppermute(value, AXES, route)


def cost(flops, nbytes):
    return pl.CostEstimate(flops=flops, bytes_accessed=nbytes, transcendentals=0)


def limit(mebibytes):
    return pltpu.CompilerParams(vmem_limit_bytes=mebibytes << 20)


def shaped(rows, width, kind):
    return jax.ShapeDtypeStruct((rows, width), kind)


def before(rows):
    down = lax.broadcasted_iota(jnp.int32, (rows, rows), 0)
    return jnp.where(down <= lax.broadcasted_iota(jnp.int32, (rows, rows), 1), 1.0, 0.0).astype(BF)


def pack_kernel(ids_ref, gates_ref, tokens_ref, out_ref):
    tokens, width = tokens_ref.shape
    weight = jnp.sum(jnp.where(ids_ref[...] == 0, gates_ref[...], 0.0), axis=0, keepdims=True)
    weight = weight.astype(BF).astype(F32)
    member = jnp.where(weight > 0, 1.0, 0.0)
    position = jnp.dot(
        jnp.broadcast_to(member, (8, tokens)).astype(BF),
        before(tokens),
        preferred_element_type=F32,
    )[:1]
    slot = lax.broadcasted_iota(jnp.int32, (CAP, tokens), 0).astype(F32)
    picked = jnp.where((position - 1.0 == slot) & (member > 0), 1.0, 0.0)
    out_ref[:, :width] = jnp.dot(
        picked.astype(BF), tokens_ref[...], preferred_element_type=F32
    ).astype(BF)
    weights = jnp.sum(picked * weight, axis=1, keepdims=True)
    out_ref[:, width:] = jnp.broadcast_to(weights, (CAP, LANES)).astype(BF)


def pack(hidden_states, expert_ids, route_gates):
    return pl.pallas_call(
        pack_kernel,
        out_shape=shaped(CAP, hidden_states.shape[1] + LANES, BF),
        compiler_params=limit(4),
    )(expert_ids.T, route_gates.T, hidden_states)


def load_kernel(gate_in, up_in, gate_ref, up_ref, sems):
    copies = [
        pltpu.make_async_copy(gate_in, gate_ref, sems.at[0]),
        pltpu.make_async_copy(up_in, up_ref, sems.at[1]),
    ]
    for copy in copies:
        copy.start()
    for copy in copies:
        copy.wait()


def load(gate_weight, up_weight):
    shape = jax.ShapeDtypeStruct(gate_weight.shape, BF)
    return pl.pallas_call(
        load_kernel,
        in_specs=[pl.BlockSpec(memory_space=pl.ANY)] * 2,
        out_specs=[VM, VM],
        out_shape=[shape, shape],
        scratch_shapes=[pltpu.SemaphoreType.DMA((2,))],
        compiler_params=limit(14),
        cost_estimate=cost(0, 4 * gate_weight.size),
    )(gate_weight, up_weight)


def gather_kernel(at_ref, *refs):
    blocks, (rows_ref, weights_ref, count_ref, all_ref) = refs[:8], refs[8:]
    total, depth = rows_ref.shape
    for k, block in enumerate(blocks):
        start = pl.multiple_of((at_ref[0] ^ k) * CAP, CAP)
        all_ref[pl.ds(start, CAP), :] = block[...]
    weights = all_ref[:, depth:]
    member = jnp.where(weights.astype(F32) > 0, 1.0, 0.0)
    count_ref[0] = jnp.sum(member[:, :1]).astype(jnp.int32)
    member = member.astype(BF)
    position = lax.dot_general(member, before(total), ROWS_OF, preferred_element_type=F32)[:1]
    down = lax.broadcasted_iota(jnp.int32, (total, total), 0)
    across = lax.broadcasted_iota(jnp.int32, (total, total), 1)
    same = jnp.where(down == across, 1.0, 0.0).astype(BF)
    member = lax.dot_general(member, same, ROWS_OF, preferred_element_type=F32)[:1]
    picked = (position - 1.0 == down.astype(F32)) & (member > 0)
    picked = jnp.where(picked, 1.0, 0.0).astype(BF)
    rows_ref[...] = jnp.dot(picked, all_ref[:, :depth], preferred_element_type=F32).astype(BF)
    weights_ref[...] = jnp.dot(picked, weights, preferred_element_type=F32).astype(BF)


def gather(at, blocks):
    rows, width = 8 * CAP, blocks[0].shape[1]
    return pl.pallas_call(
        gather_kernel,
        in_specs=[SM] + [VM] * 8,
        out_specs=[VM, VM, SM],
        out_shape=[
            shaped(rows, width - LANES, BF),
            shaped(rows, LANES, BF),
            jax.ShapeDtypeStruct((1,), jnp.int32),
        ],
        scratch_shapes=[pltpu.VMEM((rows, width), BF)],
        compiler_params=limit(6),
        cost_estimate=cost(1 << 28, 1 << 20),
    )(at, *blocks)


def project_kernel(at_ref, rows_ref, gate_ref, up_ref, *outs):
    rows = rows_ref[...]
    quarter = outs[0].shape[1] // 2
    for i, out_ref in enumerate(outs):
        units = pl.ds(pl.multiple_of(at_ref[i] * quarter, quarter), quarter)
        out_ref[:, :quarter] = jnp.dot(rows, gate_ref[:, units], preferred_element_type=F32)
        out_ref[:, quarter:] = jnp.dot(rows, up_ref[:, units], preferred_element_type=F32)


def project(at, rows, gate_weight, up_weight):
    units = gate_weight.shape[1]
    return pl.pallas_call(
        project_kernel,
        in_specs=[SM, VM, VM, VM],
        out_specs=[VM] * 4,
        out_shape=[shaped(rows.shape[0], units // 2, F32)] * 4,
        compiler_params=limit(4),
        cost_estimate=cost(4 * rows.size * units, 1 << 20),
    )(at, rows, gate_weight, up_weight)


def sum_kernel(kept_ref, got_ref, out_ref):
    out_ref[...] = (kept_ref[: out_ref.shape[0]] + got_ref[...]).astype(BF)


def add_up(kept, got):
    return pl.pallas_call(
        sum_kernel,
        in_specs=[VM, VM],
        out_specs=VM,
        out_shape=jax.ShapeDtypeStruct(got.shape, BF),
        compiler_params=limit(4),
        cost_estimate=cost(1 << 18, 1 << 20),
    )(kept, got)


def keys_kernel(kept_ref, got_ref, across_ref, out_ref):
    rows, width = out_ref.shape
    total = kept_ref[:rows] + got_ref[...] + across_ref[...].astype(F32)
    gate = total[:, :width]
    out_ref[...] = (gate / (1.0 + jnp.exp(-gate)) * total[:, width:]).astype(BF)


def keys_of(kept, got, across):
    rows, width = across.shape
    return pl.pallas_call(
        keys_kernel,
        in_specs=[VM, VM, VM],
        out_specs=VM,
        out_shape=shaped(rows, width // 2, BF),
        compiler_params=limit(6),
        cost_estimate=cost(1 << 18, 1 << 20),
    )(kept, got, across)


def assemble_kernel(at_ref, weights_ref, *refs):
    near, far, (columns_ref, panel_ref) = refs[:4], refs[4:8], refs[8:]
    rows, width = near[0].shape
    weights = weights_ref[:rows, :1].astype(F32)
    y, core, is_inside = at_ref[0], at_ref[1], at_ref[2] == 1
    for k in range(4):
        number = (y ^ (k % 2)) * 2 + (core ^ (k // 2))
        units = pl.ds(pl.multiple_of(number * width, width), width)
        keys = near[k][...]
        columns_ref[:, units] = (weights * keys.astype(F32)).astype(BF)
        panel_ref[:, units] = jnp.where(is_inside, keys, far[k][...])


def assemble(at, weights, near, far):
    rows, width = near[0].shape
    shape = shaped(rows, 4 * width, BF)
    return pl.pallas_call(
        assemble_kernel,
        in_specs=[SM] + [VM] * 9,
        out_specs=[VM, VM],
        out_shape=[shape, shape],
        compiler_params=limit(6),
        cost_estimate=cost(1 << 18, 1 << 20),
    )(at, weights, *near, *far)


SIZES = (160, 192, 224)
TILE = 256
BUFFERS = 4


def covariance_kernel(at_ref, weights_ref, columns_ref, mine_ref, *refs):
    theirs, (out_ref, buffer_ref, sems) = refs[:2], refs[-3:]
    is_home = at_ref[1] == 1
    rows, units = mine_ref.shape
    total = jnp.sum(weights_ref[:, :1].astype(F32), axis=0, keepdims=True)
    scale = 1.0 / total
    steps = units // TILE

    def copy(i):
        start = pl.multiple_of(at_ref[0] * units + i * TILE, TILE)
        slot = i % BUFFERS
        return pltpu.make_async_copy(
            buffer_ref.at[slot], out_ref.at[pl.ds(start, TILE)], sems.at[slot]
        )

    for i in range(steps):
        at = i * TILE
        their_ref = theirs[0]
        part = slice(at, at + TILE)
        if at >= theirs[0].shape[1]:
            their_ref = theirs[1]
            part = slice(at - theirs[0].shape[1], at - theirs[0].shape[1] + TILE)
        panel = jnp.where(is_home, mine_ref[:, at : at + TILE], their_ref[:, part])
        if i >= BUFFERS:
            copy(i - BUFFERS).wait()
        value = lax.dot_general(panel, columns_ref[...], ROWS_OF, preferred_element_type=F32)
        buffer_ref[i % BUFFERS] = value * scale
        copy(i).start()
    for i in range(steps - BUFFERS, steps):
        copy(i).wait()


def covariance_part(at, weights, columns, mine, theirs, out_rows, into):
    rows, units = mine.shape
    width = columns.shape[1]
    if len(theirs) == 1:
        theirs = theirs * 2
    args = [at, weights, columns, mine, *theirs]
    in_specs = [SM] + [VM] * 5
    aliases = {}
    if into is not None:
        args.append(into)
        in_specs.append(pl.BlockSpec(memory_space=pl.ANY))
        aliases = {6: 0}
    return pl.pallas_call(
        covariance_kernel,
        in_specs=in_specs,
        out_specs=pl.BlockSpec(memory_space=pl.ANY),
        out_shape=shaped(out_rows, width, F32),
        scratch_shapes=[
            pltpu.VMEM((BUFFERS, TILE, width), F32),
            pltpu.SemaphoreType.DMA((BUFFERS,)),
        ],
        input_output_aliases=aliases,
        compiler_params=limit(14),
        cost_estimate=cost(2 * rows * units * width, 4 * units * width),
    )(*args)


def numbers(*values):
    return jnp.stack([jnp.asarray(v, jnp.int32) for v in values])


def fast(hidden_states, expert_ids, route_gates, gate_weight, up_weight):
    units = gate_weight.shape[1]
    dp, tensor = lax.axis_index("dp"), lax.axis_index("tensor")
    z, x, y, core = dp // 2, dp % 2, tensor // 2, tensor % 2
    is_home, is_inside = core == z % 2, y == z // 2
    quarters = [(1 - y, 1 - core), (y, 1 - core), (1 - y, core), (y, core)]
    project_at = numbers(*[of_y * 2 + of_core for of_y, of_core in quarters])
    half_at = [numbers(x, is_home), numbers(1 - x, is_home)]
    keys_at = numbers(y, core, is_inside)

    def beside(mine):
        return [mine, send(mine, X), send(mine, Z1), send(mine, XZ1)]

    def rest(rows, weights, given_across, given, kept_across, kept):
        across = add_up(kept_across, send(given_across[:rows], CORE))
        arrived = send(across, Y)
        keys = keys_of(kept, send(given[:rows], CORE), arrived)
        far = [send(keys, FAR)]
        swapped = send(keys, CORE)
        keys, swapped = lax.optimization_barrier((keys, swapped))
        far.append(send(keys, FAR_Y))
        near = [keys, send(keys, Y)]
        near += [swapped, send(near[1], CORE)]
        far += [send(k, CORE) for k in far]
        columns, panel = assemble(keys_at, weights, near, far)
        shared = send(panel, SHARE)
        cut = units * 6 // 8
        last = [send(shared[:, :cut], AWAY_X), send(shared[:, cut:], HOME_Z1)]
        out = covariance_part(half_at[0], weights, columns, panel, [shared], 2 * units, None)
        return covariance_part(half_at[1], weights, columns, shared, last, 2 * units, out)

    own = pack(hidden_states, expert_ids, route_gates)
    far = send(own, Z2)
    far, gate_weight, up_weight = lax.optimization_barrier((far, gate_weight, up_weight))
    gate_weight, up_weight = load(gate_weight, up_weight)
    blocks = beside(own) + beside(far)
    rows, weights, count = gather(numbers(dp), blocks)
    parts = project(project_at, rows, gate_weight, up_weight)
    sizes = [r for r in SIZES if r < rows.shape[0]] + [rows.shape[0]]
    branch = sum((count[0] > r).astype(jnp.int32) for r in sizes[:-1])
    return lax.switch(
        branch, [functools.partial(rest, r) for r in sizes], weights, *parts
    )


def solution(mesh):
    placed = (P("dp", "tensor"), P("dp", None), P("dp", None), P("tensor", "dp"), P("tensor", "dp"))
    sizes = (mesh.shape["dp"], mesh.shape["tensor"])
    return jax.shard_map(
        fast if sizes == (8, 4) else any_mesh,
        mesh=mesh,
        in_specs=placed,
        out_specs=P("tensor", "dp"),
        check_vma=False,
    )
```

```python
import functools

import jax
import jax.numpy as jnp
from jax import lax
from jax.experimental import pallas as pl
from jax.experimental.pallas import tpu as pltpu
from jax.sharding import PartitionSpec as P

CAP = 32
LANES = 128
BF, F32 = jnp.bfloat16, jnp.float32
AXES = ("dp", "tensor")
ROWS_OF = (((0,), (0,)), ((), ()))


def pack_rows(token_blocks, weight_blocks):
    member = (weight_blocks > 0).astype(jnp.int32)
    position = jnp.cumsum(member, axis=1) - 1
    slot_index = lax.broadcasted_iota(jnp.int32, (1, CAP, 1), 1)
    picked = (position[:, None, :] == slot_index) & (member[:, None, :] > 0)
    selector = picked.astype(BF)
    packed = jnp.einsum(
        "sct,std->scd", selector, token_blocks, preferred_element_type=F32
    ).astype(BF)
    packed_weight = jnp.einsum(
        "sct,st->sc", selector, weight_blocks, preferred_element_type=F32
    ).astype(BF)
    return (packed.reshape(-1, token_blocks.shape[2]), packed_weight.reshape(-1))


def any_mesh(hidden_states, expert_ids, route_gates, gate_weight, up_weight):
    route_weight = jnp.sum(
        jnp.where(expert_ids == 0, route_gates, jnp.zeros_like(route_gates)), axis=1
    ).astype(BF)
    own_rows, own_weight = pack_rows(hidden_states[None], route_weight[None])
    packed_rows, packed_weight = (
        lax.all_gather(own_rows, "dp", axis=0, tiled=True),
        lax.all_gather(own_weight, "dp", axis=0, tiled=True),
    )
    weight_total = jnp.sum(packed_weight.astype(F32))
    gate_part = jnp.dot(packed_rows, gate_weight, preferred_element_type=F32)
    up_part = jnp.dot(packed_rows, up_weight, preferred_element_type=F32)
    summed = lax.psum_scatter(
        jnp.concatenate([gate_part, up_part], axis=1), "tensor", scatter_dimension=0, tiled=True
    )
    unit_width = gate_weight.shape[1]
    local_keys = (jax.nn.silu(summed[:, :unit_width]) * summed[:, unit_width:]).astype(BF)
    column_keys = lax.all_gather(local_keys, "tensor", axis=0, tiled=True)
    weighted = (packed_weight.astype(F32)[:, None] * column_keys.astype(F32)).astype(BF)
    spread_keys = lax.all_gather(local_keys, "dp", axis=1, tiled=True)
    row_keys = lax.all_to_all(spread_keys, "tensor", split_axis=1, concat_axis=0, tiled=True)
    covariance = lax.dot_general(row_keys, weighted, ROWS_OF, preferred_element_type=F32)
    return covariance / weight_total


def pairs(to):
    number = lambda z, x, y, c: z * 8 + x * 4 + y * 2 + c
    out = []
    for z in range(4):
        for x in range(2):
            for y in range(2):
                for c in range(2):
                    there = to(z, x, y, c)
                    if there is not None:
                        out.append((number(z, x, y, c), number(*there)))
    return out


def inside(z, y):
    return z // 2 == y


CORE = pairs(lambda z, x, y, c: (z, x, y, 1 - c))
Y = pairs(lambda z, x, y, c: (z, x, 1 - y, c))
X = pairs(lambda z, x, y, c: (z, 1 - x, y, c))
Z1 = pairs(lambda z, x, y, c: (z ^ 1, x, y, c))
Z2 = pairs(lambda z, x, y, c: (z ^ 2, x, y, c))
XZ1 = pairs(lambda z, x, y, c: (z ^ 1, 1 - x, y, c))
FAR = pairs(lambda z, x, y, c: (z ^ 2, x, y, c) if inside(z, y) else None)
FAR_Y = pairs(lambda z, x, y, c: (z ^ 2, x, 1 - y, c) if not inside(z, y) else None)
SHARE = pairs(lambda z, x, y, c: (z ^ 1, x, y, c) if c == z % 2 else (z, 1 - x, y, 1 - c))
CROSS = pairs(lambda z, x, y, c: (z ^ 1, 1 - x, y, c) if c == z % 2 else None)

VM = pl.BlockSpec(memory_space=pltpu.VMEM)
SM = pl.BlockSpec(memory_space=pltpu.SMEM)


def send(value, route):
    return lax.ppermute(value, AXES, route)


def cost(flops, nbytes):
    return pl.CostEstimate(flops=flops, bytes_accessed=nbytes, transcendentals=0)


def limit(mebibytes):
    return pltpu.CompilerParams(vmem_limit_bytes=mebibytes << 20)


def shaped(rows, width, kind):
    return jax.ShapeDtypeStruct((rows, width), kind)


def before(rows):
    down = lax.broadcasted_iota(jnp.int32, (rows, rows), 0)
    return jnp.where(down <= lax.broadcasted_iota(jnp.int32, (rows, rows), 1), 1.0, 0.0).astype(BF)


def pack_kernel(ids_ref, gates_ref, tokens_ref, out_ref):
    tokens, width = tokens_ref.shape
    weight = jnp.sum(jnp.where(ids_ref[...] == 0, gates_ref[...], 0.0), axis=0, keepdims=True)
    weight = weight.astype(BF).astype(F32)
    member = jnp.where(weight > 0, 1.0, 0.0)
    position = jnp.dot(
        jnp.broadcast_to(member, (8, tokens)).astype(BF),
        before(tokens),
        preferred_element_type=F32,
    )[:1]
    slot = lax.broadcasted_iota(jnp.int32, (CAP, tokens), 0).astype(F32)
    picked = jnp.where((position - 1.0 == slot) & (member > 0), 1.0, 0.0)
    out_ref[:, :width] = jnp.dot(
        picked.astype(BF), tokens_ref[...], preferred_element_type=F32
    ).astype(BF)
    weights = jnp.sum(picked * weight, axis=1, keepdims=True)
    out_ref[:, width:] = jnp.broadcast_to(weights, (CAP, LANES)).astype(BF)


def pack(hidden_states, expert_ids, route_gates):
    return pl.pallas_call(
        pack_kernel,
        out_shape=shaped(CAP, hidden_states.shape[1] + LANES, BF),
    )(expert_ids.T, route_gates.T, hidden_states)


def load_kernel(gate_in, up_in, gate_ref, up_ref, sems):
    copies = [
        pltpu.make_async_copy(gate_in, gate_ref, sems.at[0]),
        pltpu.make_async_copy(up_in, up_ref, sems.at[1]),
    ]
    for copy in copies:
        copy.start()
    for copy in copies:
        copy.wait()


def load(gate_weight, up_weight):
    shape = jax.ShapeDtypeStruct(gate_weight.shape, BF)
    return pl.pallas_call(
        load_kernel,
        in_specs=[pl.BlockSpec(memory_space=pl.ANY)] * 2,
        out_specs=[VM, VM],
        out_shape=[shape, shape],
        scratch_shapes=[pltpu.SemaphoreType.DMA((2,))],
        compiler_params=limit(14),
        cost_estimate=cost(0, 4 * gate_weight.size),
    )(gate_weight, up_weight)


def gather_kernel(sizes, at_ref, *refs):
    blocks, (rows_ref, weights_ref, branch_ref, all_ref) = refs[:8], refs[8:]
    total, depth = rows_ref.shape
    for k, block in enumerate(blocks):
        start = pl.multiple_of((at_ref[0] ^ k) * CAP, CAP)
        all_ref[pl.ds(start, CAP), :] = block[...]
    weights = all_ref[:, depth:]
    member = jnp.where(weights.astype(F32) > 0, 1.0, 0.0)
    count = jnp.sum(member[:, :1])
    branch_ref[0] = sum((count > size).astype(jnp.int32) for size in sizes[:-1])
    member = member.astype(BF)
    position = lax.dot_general(member, before(total), ROWS_OF, preferred_element_type=F32)[:1]
    down = lax.broadcasted_iota(jnp.int32, (total, total), 0)
    across = lax.broadcasted_iota(jnp.int32, (total, total), 1)
    same = jnp.where(down == across, 1.0, 0.0).astype(BF)
    member = lax.dot_general(member, same, ROWS_OF, preferred_element_type=F32)[:1]
    picked = (position - 1.0 == down.astype(F32)) & (member > 0)
    picked = jnp.where(picked, 1.0, 0.0).astype(BF)
    rows_ref[...] = jnp.dot(picked, all_ref[:, :depth], preferred_element_type=F32).astype(BF)
    weights_ref[...] = jnp.dot(picked, weights, preferred_element_type=F32).astype(BF)


def gather(at, blocks, sizes):
    rows, width = 8 * CAP, blocks[0].shape[1]
    return pl.pallas_call(
        functools.partial(gather_kernel, sizes),
        in_specs=[SM] + [VM] * 8,
        out_specs=[VM, VM, SM],
        out_shape=[
            shaped(rows, width - LANES, BF),
            shaped(rows, LANES, BF),
            jax.ShapeDtypeStruct((1,), jnp.int32),
        ],
        scratch_shapes=[pltpu.VMEM((rows, width), BF)],
        compiler_params=limit(6),
        cost_estimate=cost(1 << 28, 1 << 20),
    )(at, *blocks)


def project_kernel(at_ref, rows_ref, gate_ref, up_ref, *outs):
    rows = rows_ref[...]
    quarter = outs[0].shape[1] // 2
    for i, out_ref in enumerate(outs):
        units = pl.ds(pl.multiple_of(at_ref[i] * quarter, quarter), quarter)
        out_ref[:, :quarter] = jnp.dot(rows, gate_ref[:, units], preferred_element_type=F32)
        out_ref[:, quarter:] = jnp.dot(rows, up_ref[:, units], preferred_element_type=F32)


def project(at, rows, gate_weight, up_weight):
    units = gate_weight.shape[1]
    return pl.pallas_call(
        project_kernel,
        in_specs=[SM, VM, VM, VM],
        out_specs=[VM] * 4,
        out_shape=[shaped(rows.shape[0], units // 2, F32)] * 4,
        compiler_params=limit(4),
        cost_estimate=cost(4 * rows.size * units, 1 << 20),
    )(at, rows, gate_weight, up_weight)


def sum_kernel(kept_ref, got_ref, out_ref):
    out_ref[...] = (kept_ref[: out_ref.shape[0]] + got_ref[...]).astype(BF)


def add_up(kept, got):
    return pl.pallas_call(
        sum_kernel,
        in_specs=[VM, VM],
        out_specs=VM,
        out_shape=jax.ShapeDtypeStruct(got.shape, BF),
        compiler_params=limit(4),
        cost_estimate=cost(1 << 18, 1 << 20),
    )(kept, got)


def keys_kernel(kept_ref, got_ref, across_ref, out_ref):
    rows, width = out_ref.shape
    total = kept_ref[:rows] + got_ref[...] + across_ref[...].astype(F32)
    gate = total[:, :width]
    out_ref[...] = (gate / (1.0 + jnp.exp(-gate)) * total[:, width:]).astype(BF)


def keys_of(kept, got, across):
    rows, width = across.shape
    return pl.pallas_call(
        keys_kernel,
        in_specs=[VM, VM, VM],
        out_specs=VM,
        out_shape=shaped(rows, width // 2, BF),
        compiler_params=limit(6),
        cost_estimate=cost(1 << 18, 1 << 20),
    )(kept, got, across)


def assemble_kernel(at_ref, weights_ref, *refs):
    near, far, (columns_ref, panel_ref) = refs[:4], refs[4:8], refs[8:]
    rows, width = near[0].shape
    weights = weights_ref[:rows, :1].astype(F32)
    y, core, is_inside = at_ref[0], at_ref[1], at_ref[2] == 1
    for k in range(4):
        number = (y ^ (k % 2)) * 2 + (core ^ (k // 2))
        units = pl.ds(pl.multiple_of(number * width, width), width)
        keys = near[k][...]
        columns_ref[:, units] = (weights * keys.astype(F32)).astype(BF)
        panel_ref[:, units] = jnp.where(is_inside, keys, far[k][...])


def assemble(at, weights, near, far):
    rows, width = near[0].shape
    shape = shaped(rows, 4 * width, BF)
    return pl.pallas_call(
        assemble_kernel,
        in_specs=[SM] + [VM] * 9,
        out_specs=[VM, VM],
        out_shape=[shape, shape],
        compiler_params=limit(6),
        cost_estimate=cost(1 << 18, 1 << 20),
    )(at, weights, *near, *far)


SIZES = (128, 144, 160, 176, 192, 208, 224)
TILE = 256
BUFFERS = 4


def covariance_kernel(at_ref, weights_ref, columns_ref, panel_ref, *refs):
    out_ref, buffer_ref, sems = refs[-3:]
    units = panel_ref.shape[1]
    steps = units // TILE

    def copy(i):
        start = pl.multiple_of(at_ref[0] * units + i * TILE, TILE)
        slot = lax.rem(i, BUFFERS)
        return pltpu.make_async_copy(
            buffer_ref.at[slot], out_ref.at[pl.ds(start, TILE)], sems.at[slot]
        )

    @pl.when(at_ref[1] == 1)
    def _():
        total = jnp.sum(weights_ref[:, :1].astype(F32), axis=0, keepdims=True)
        scale = 1.0 / total

        def step(i, carry):
            @pl.when(i >= BUFFERS)
            def _():
                copy(i - BUFFERS).wait()

            part = panel_ref[:, pl.ds(pl.multiple_of(i * TILE, TILE), TILE)]
            value = lax.dot_general(part, columns_ref[...], ROWS_OF, preferred_element_type=F32)
            buffer_ref[lax.rem(i, BUFFERS)] = value * scale
            copy(i).start()
            return carry

        lax.fori_loop(0, steps, step, 0)

        def finish(i, carry):
            copy(i).wait()
            return carry

        lax.fori_loop(steps - BUFFERS, steps, finish, 0)


def covariance_part(at, weights, columns, panel, out_rows, into):
    rows, units = panel.shape
    width = columns.shape[1]
    args = [at, weights, columns, panel]
    in_specs = [SM, VM, VM, VM]
    aliases = {}
    if into is not None:
        args.append(into)
        in_specs.append(pl.BlockSpec(memory_space=pl.ANY))
        aliases = {4: 0}
    return pl.pallas_call(
        covariance_kernel,
        in_specs=in_specs,
        out_specs=pl.BlockSpec(memory_space=pl.ANY),
        out_shape=shaped(out_rows, width, F32),
        scratch_shapes=[
            pltpu.VMEM((BUFFERS, TILE, width), F32),
            pltpu.SemaphoreType.DMA((BUFFERS,)),
        ],
        input_output_aliases=aliases,
        compiler_params=limit(14),
        cost_estimate=cost(2 * rows * units * width, 4 * units * width),
    )(*args)


def numbers(*values):
    return jnp.stack([jnp.asarray(v, jnp.int32) for v in values])


def fast(hidden_states, expert_ids, route_gates, gate_weight, up_weight):
    units = gate_weight.shape[1]
    dp, tensor = lax.axis_index("dp"), lax.axis_index("tensor")
    z, x, y, core = dp // 2, dp % 2, tensor // 2, tensor % 2
    is_home, is_inside = core == z % 2, y == z // 2
    quarters = [(1 - y, 1 - core), (y, 1 - core), (1 - y, core), (y, core)]
    project_at = numbers(*[of_y * 2 + of_core for of_y, of_core in quarters])
    mine_at = numbers(x, is_home)
    shared_at = numbers(jnp.where(is_home, 1 - x, x), 1)
    last_at = numbers(1 - x, core != z % 2)
    keys_at = numbers(y, core, is_inside)

    def beside(mine):
        return [mine, send(mine, X), send(mine, Z1), send(mine, XZ1)]

    def rest(rows, weights, given_across, given, kept_across, kept):
        across = add_up(kept_across, send(given_across[:rows], CORE))
        arrived = send(across, Y)
        keys = keys_of(kept, send(given[:rows], CORE), arrived)
        far = [send(keys, FAR)]
        swapped = send(keys, CORE)
        keys, swapped = lax.optimization_barrier((keys, swapped))
        far.append(send(keys, FAR_Y))
        near = [keys, send(keys, Y)]
        near += [swapped, send(near[1], CORE)]
        far += [send(k, CORE) for k in far]
        columns, panel = assemble(keys_at, weights, near, far)
        shared = send(panel, SHARE)
        last = send(panel, CROSS)
        out = covariance_part(mine_at, weights, columns, panel, 2 * units, None)
        out = covariance_part(shared_at, weights, columns, shared, 2 * units, out)
        return covariance_part(last_at, weights, columns, last, 2 * units, out)

    own = pack(hidden_states, expert_ids, route_gates)
    far = send(own, Z2)
    far, gate_weight, up_weight = lax.optimization_barrier((far, gate_weight, up_weight))
    gate_weight, up_weight = load(gate_weight, up_weight)
    blocks = beside(own) + beside(far)
    sizes = [size for size in SIZES if size < 8 * CAP] + [8 * CAP]
    rows, weights, branch = gather(numbers(dp), blocks, sizes)
    parts = project(project_at, rows, gate_weight, up_weight)
    return lax.switch(
        branch[0], [functools.partial(rest, size) for size in sizes], weights, *parts
    )


def solution(mesh):
    placed = (P("dp", "tensor"), P("dp", None), P("dp", None), P("tensor", "dp"), P("tensor", "dp"))
    sizes = (mesh.shape["dp"], mesh.shape["tensor"])
    return jax.shard_map(
        fast if sizes == (8, 4) else any_mesh,
        mesh=mesh,
        in_specs=placed,
        out_specs=P("tensor", "dp"),
        check_vma=False,
    )
```

```python
import functools

import jax
import jax.numpy as jnp
from jax import lax
from jax.experimental import pallas as pl
from jax.experimental.pallas import tpu as pltpu
from jax.sharding import PartitionSpec as P

CAP = 32
LANES = 128
BF, F32 = jnp.bfloat16, jnp.float32
AXES = ("dp", "tensor")
ROWS_OF = (((0,), (0,)), ((), ()))


def pack_rows(token_blocks, weight_blocks):
    member = (weight_blocks > 0).astype(jnp.int32)
    position = jnp.cumsum(member, axis=1) - 1
    slot_index = lax.broadcasted_iota(jnp.int32, (1, CAP, 1), 1)
    picked = (position[:, None, :] == slot_index) & (member[:, None, :] > 0)
    selector = picked.astype(BF)
    packed = jnp.einsum(
        "sct,std->scd", selector, token_blocks, preferred_element_type=F32
    ).astype(BF)
    packed_weight = jnp.einsum(
        "sct,st->sc", selector, weight_blocks, preferred_element_type=F32
    ).astype(BF)
    return (packed.reshape(-1, token_blocks.shape[2]), packed_weight.reshape(-1))


def any_mesh(hidden_states, expert_ids, route_gates, gate_weight, up_weight):
    route_weight = jnp.sum(
        jnp.where(expert_ids == 0, route_gates, jnp.zeros_like(route_gates)), axis=1
    ).astype(BF)
    own_rows, own_weight = pack_rows(hidden_states[None], route_weight[None])
    packed_rows, packed_weight = (
        lax.all_gather(own_rows, "dp", axis=0, tiled=True),
        lax.all_gather(own_weight, "dp", axis=0, tiled=True),
    )
    weight_total = jnp.sum(packed_weight.astype(F32))
    gate_part = jnp.dot(packed_rows, gate_weight, preferred_element_type=F32)
    up_part = jnp.dot(packed_rows, up_weight, preferred_element_type=F32)
    summed = lax.psum_scatter(
        jnp.concatenate([gate_part, up_part], axis=1), "tensor", scatter_dimension=0, tiled=True
    )
    unit_width = gate_weight.shape[1]
    local_keys = (jax.nn.silu(summed[:, :unit_width]) * summed[:, unit_width:]).astype(BF)
    column_keys = lax.all_gather(local_keys, "tensor", axis=0, tiled=True)
    weighted = (packed_weight.astype(F32)[:, None] * column_keys.astype(F32)).astype(BF)
    spread_keys = lax.all_gather(local_keys, "dp", axis=1, tiled=True)
    row_keys = lax.all_to_all(spread_keys, "tensor", split_axis=1, concat_axis=0, tiled=True)
    covariance = lax.dot_general(row_keys, weighted, ROWS_OF, preferred_element_type=F32)
    return covariance / weight_total


def pairs(to):
    number = lambda z, x, y, c: z * 8 + x * 4 + y * 2 + c
    out = []
    for z in range(4):
        for x in range(2):
            for y in range(2):
                for c in range(2):
                    there = to(z, x, y, c)
                    if there is not None:
                        out.append((number(z, x, y, c), number(*there)))
    return out


def inside(z, y):
    return z // 2 == y


CORE = pairs(lambda z, x, y, c: (z, x, y, 1 - c))
Y = pairs(lambda z, x, y, c: (z, x, 1 - y, c))
X = pairs(lambda z, x, y, c: (z, 1 - x, y, c))
Z1 = pairs(lambda z, x, y, c: (z ^ 1, x, y, c))
Z2 = pairs(lambda z, x, y, c: (z ^ 2, x, y, c))
XZ1 = pairs(lambda z, x, y, c: (z ^ 1, 1 - x, y, c))
FAR = pairs(lambda z, x, y, c: (z ^ 2, x, y, c) if inside(z, y) else None)
FAR_Y = pairs(lambda z, x, y, c: (z ^ 2, x, 1 - y, c) if not inside(z, y) else None)
SHARE = pairs(lambda z, x, y, c: (z ^ 1, x, y, c) if c == z % 2 else (z, 1 - x, y, 1 - c))
CROSS = pairs(lambda z, x, y, c: (z ^ 1, 1 - x, y, c) if c == z % 2 else None)

VM = pl.BlockSpec(memory_space=pltpu.VMEM)
SM = pl.BlockSpec(memory_space=pltpu.SMEM)


def send(value, route):
    return lax.ppermute(value, AXES, route)


def cost(flops, nbytes):
    return pl.CostEstimate(flops=flops, bytes_accessed=nbytes, transcendentals=0)


def limit(mebibytes):
    return pltpu.CompilerParams(vmem_limit_bytes=mebibytes << 20)


def shaped(rows, width, kind):
    return jax.ShapeDtypeStruct((rows, width), kind)


def before(rows):
    down = lax.broadcasted_iota(jnp.int32, (rows, rows), 0)
    return jnp.where(down <= lax.broadcasted_iota(jnp.int32, (rows, rows), 1), 1.0, 0.0).astype(BF)


def pack_kernel(ids_ref, gates_ref, tokens_ref, out_ref):
    tokens, width = tokens_ref.shape
    weight = jnp.sum(jnp.where(ids_ref[...] == 0, gates_ref[...], 0.0), axis=0, keepdims=True)
    weight = weight.astype(BF).astype(F32)
    member = jnp.where(weight > 0, 1.0, 0.0)
    position = jnp.dot(
        jnp.broadcast_to(member, (8, tokens)).astype(BF),
        before(tokens),
        preferred_element_type=F32,
    )[:1]
    slot = lax.broadcasted_iota(jnp.int32, (CAP, tokens), 0).astype(F32)
    picked = jnp.where((position - 1.0 == slot) & (member > 0), 1.0, 0.0)
    out_ref[:, :width] = jnp.dot(
        picked.astype(BF), tokens_ref[...], preferred_element_type=F32
    ).astype(BF)
    weights = jnp.sum(picked * weight, axis=1, keepdims=True)
    out_ref[:, width:] = jnp.broadcast_to(weights, (CAP, LANES)).astype(BF)


def pack(hidden_states, expert_ids, route_gates):
    return pl.pallas_call(
        pack_kernel,
        out_shape=shaped(CAP, hidden_states.shape[1] + LANES, BF),
        compiler_params=limit(4),
    )(expert_ids.T, route_gates.T, hidden_states)


def load_kernel(weight_in, weight_ref, sem):
    copy = pltpu.make_async_copy(weight_in, weight_ref, sem)
    copy.start()
    copy.wait()


def load(weight):
    return pl.pallas_call(
        load_kernel,
        in_specs=[pl.BlockSpec(memory_space=pl.ANY)],
        out_specs=VM,
        out_shape=jax.ShapeDtypeStruct(weight.shape, BF),
        scratch_shapes=[pltpu.SemaphoreType.DMA],
        compiler_params=limit(44),
        cost_estimate=cost(0, 2 * weight.size),
    )(weight)


def gather_kernel(sizes, at_ref, *refs):
    blocks, (rows_ref, weights_ref, branch_ref, all_ref) = refs[:8], refs[8:]
    total, depth = rows_ref.shape
    for k, block in enumerate(blocks):
        start = pl.multiple_of((at_ref[0] ^ k) * CAP, CAP)
        all_ref[pl.ds(start, CAP), :] = block[...]
    weights = all_ref[:, depth:]
    member = jnp.where(weights.astype(F32) > 0, 1.0, 0.0)
    count = jnp.sum(member[:, :1])
    branch_ref[0] = sum((count > size).astype(jnp.int32) for size in sizes[:-1])
    member = member.astype(BF)
    position = lax.dot_general(member, before(total), ROWS_OF, preferred_element_type=F32)[:1]
    down = lax.broadcasted_iota(jnp.int32, (total, total), 0)
    across = lax.broadcasted_iota(jnp.int32, (total, total), 1)
    same = jnp.where(down == across, 1.0, 0.0).astype(BF)
    member = lax.dot_general(member, same, ROWS_OF, preferred_element_type=F32)[:1]
    picked = (position - 1.0 == down.astype(F32)) & (member > 0)
    picked = jnp.where(picked, 1.0, 0.0).astype(BF)
    rows_ref[...] = jnp.dot(picked, all_ref[:, :depth], preferred_element_type=F32).astype(BF)
    weights_ref[...] = jnp.dot(picked, weights, preferred_element_type=F32).astype(BF)


def gather(at, blocks, sizes):
    rows, width = 8 * CAP, blocks[0].shape[1]
    return pl.pallas_call(
        functools.partial(gather_kernel, sizes),
        in_specs=[SM] + [VM] * 8,
        out_specs=[VM, VM, SM],
        out_shape=[
            shaped(rows, width - LANES, BF),
            shaped(rows, LANES, BF),
            jax.ShapeDtypeStruct((1,), jnp.int32),
        ],
        scratch_shapes=[pltpu.VMEM((rows, width), BF)],
        compiler_params=limit(6),
        cost_estimate=cost(1 << 28, 1 << 20),
    )(at, *blocks)


def project_kernel(at_ref, rows_ref, gate_ref, up_ref, *outs):
    rows = rows_ref[...]
    quarter = outs[0].shape[1] // 2
    for i, out_ref in enumerate(outs):
        units = pl.ds(pl.multiple_of(at_ref[i] * quarter, quarter), quarter)
        out_ref[:, :quarter] = jnp.dot(rows, gate_ref[:, units], preferred_element_type=F32)
        out_ref[:, quarter:] = jnp.dot(rows, up_ref[:, units], preferred_element_type=F32)


def project(at, rows, gate_weight, up_weight):
    units = gate_weight.shape[1]
    return pl.pallas_call(
        project_kernel,
        in_specs=[SM, VM, VM, VM],
        out_specs=[VM] * 4,
        out_shape=[shaped(rows.shape[0], units // 2, F32)] * 4,
        compiler_params=limit(4),
        cost_estimate=cost(4 * rows.size * units, 1 << 20),
    )(at, rows, gate_weight, up_weight)


def sum_kernel(kept_ref, got_ref, out_ref):
    out_ref[...] = (kept_ref[: out_ref.shape[0]] + got_ref[...]).astype(BF)


def add_up(kept, got):
    return pl.pallas_call(
        sum_kernel,
        in_specs=[VM, VM],
        out_specs=VM,
        out_shape=jax.ShapeDtypeStruct(got.shape, BF),
        compiler_params=limit(4),
        cost_estimate=cost(1 << 18, 1 << 20),
    )(kept, got)


def keys_kernel(kept_ref, got_ref, across_ref, out_ref):
    rows, width = out_ref.shape
    total = kept_ref[:rows] + got_ref[...] + across_ref[...].astype(F32)
    gate = total[:, :width]
    out_ref[...] = (gate / (1.0 + jnp.exp(-gate)) * total[:, width:]).astype(BF)


def keys_of(kept, got, across):
    rows, width = across.shape
    return pl.pallas_call(
        keys_kernel,
        in_specs=[VM, VM, VM],
        out_specs=VM,
        out_shape=shaped(rows, width // 2, BF),
        compiler_params=limit(6),
        cost_estimate=cost(1 << 18, 1 << 20),
    )(kept, got, across)


def assemble_kernel(at_ref, weights_ref, *refs):
    near, far, (columns_ref, panel_ref) = refs[:4], refs[4:8], refs[8:]
    rows, width = near[0].shape
    weights = weights_ref[:rows, :1].astype(F32)
    y, core, is_inside = at_ref[0], at_ref[1], at_ref[2] == 1
    for k in range(4):
        number = (y ^ (k % 2)) * 2 + (core ^ (k // 2))
        units = pl.ds(pl.multiple_of(number * width, width), width)
        keys = near[k][...]
        columns_ref[:, units] = (weights * keys.astype(F32)).astype(BF)
        panel_ref[:, units] = jnp.where(is_inside, keys, far[k][...])


def assemble(at, weights, near, far):
    rows, width = near[0].shape
    shape = shaped(rows, 4 * width, BF)
    return pl.pallas_call(
        assemble_kernel,
        in_specs=[SM] + [VM] * 9,
        out_specs=[VM, VM],
        out_shape=[shape, shape],
        compiler_params=limit(6),
        cost_estimate=cost(1 << 18, 1 << 20),
    )(at, weights, *near, *far)


SIZES = (128, 144, 160, 176, 192, 208, 224)
TILE = 256
BUFFERS = 4


def covariance_kernel(at_ref, weights_ref, columns_ref, panel_ref, *refs):
    out_ref, buffer_ref, sems = refs[-3:]
    units = panel_ref.shape[1]
    steps = units // TILE

    def copy(i):
        start = pl.multiple_of(at_ref[0] * units + i * TILE, TILE)
        slot = lax.rem(i, BUFFERS)
        return pltpu.make_async_copy(
            buffer_ref.at[slot], out_ref.at[pl.ds(start, TILE)], sems.at[slot]
        )

    @pl.when(at_ref[1] == 1)
    def _():
        total = jnp.sum(weights_ref[:, :1].astype(F32), axis=0, keepdims=True)
        scale = 1.0 / total

        def step(i, carry):
            @pl.when(i >= BUFFERS)
            def _():
                copy(i - BUFFERS).wait()

            part = panel_ref[:, pl.ds(pl.multiple_of(i * TILE, TILE), TILE)]
            value = lax.dot_general(part, columns_ref[...], ROWS_OF, preferred_element_type=F32)
            buffer_ref[lax.rem(i, BUFFERS)] = value * scale
            copy(i).start()
            return carry

        lax.fori_loop(0, steps, step, 0)

        def finish(i, carry):
            copy(i).wait()
            return carry

        lax.fori_loop(steps - BUFFERS, steps, finish, 0)


def covariance_part(at, weights, columns, panel, out_rows, into):
    rows, units = panel.shape
    width = columns.shape[1]
    args = [at, weights, columns, panel]
    in_specs = [SM, VM, VM, VM]
    aliases = {}
    if into is not None:
        args.append(into)
        in_specs.append(pl.BlockSpec(memory_space=pl.ANY))
        aliases = {4: 0}
    return pl.pallas_call(
        covariance_kernel,
        in_specs=in_specs,
        out_specs=pl.BlockSpec(memory_space=pl.ANY),
        out_shape=shaped(out_rows, width, F32),
        scratch_shapes=[
            pltpu.VMEM((BUFFERS, TILE, width), F32),
            pltpu.SemaphoreType.DMA((BUFFERS,)),
        ],
        input_output_aliases=aliases,
        compiler_params=limit(14),
        cost_estimate=cost(2 * rows * units * width, 4 * units * width),
    )(*args)


def numbers(*values):
    return jnp.stack([jnp.asarray(v, jnp.int32) for v in values])


def fast(hidden_states, expert_ids, route_gates, gate_weight, up_weight):
    units = gate_weight.shape[1]
    dp, tensor = lax.axis_index("dp"), lax.axis_index("tensor")
    z, x, y, core = dp // 2, dp % 2, tensor // 2, tensor % 2
    is_home, is_inside = core == z % 2, y == z // 2
    quarters = [(1 - y, 1 - core), (y, 1 - core), (1 - y, core), (y, core)]
    project_at = numbers(*[of_y * 2 + of_core for of_y, of_core in quarters])
    mine_at = numbers(x, is_home)
    shared_at = numbers(jnp.where(is_home, 1 - x, x), 1)
    last_at = numbers(1 - x, core != z % 2)
    keys_at = numbers(y, core, is_inside)

    def beside(mine):
        return [mine, send(mine, X), send(mine, Z1), send(mine, XZ1)]

    def rest(rows, weights, given_across, given, kept_across, kept):
        across = add_up(kept_across, send(given_across[:rows], CORE))
        arrived = send(across, Y)
        keys = keys_of(kept, send(given[:rows], CORE), arrived)
        far = [send(keys, FAR)]
        swapped = send(keys, CORE)
        keys, swapped = lax.optimization_barrier((keys, swapped))
        far.append(send(keys, FAR_Y))
        near = [keys, send(keys, Y)]
        near += [swapped, send(near[1], CORE)]
        far += [send(k, CORE) for k in far]
        columns, panel = assemble(keys_at, weights, near, far)
        shared = send(panel, SHARE)
        last = send(panel, CROSS)
        out = covariance_part(mine_at, weights, columns, panel, 2 * units, None)
        out = covariance_part(shared_at, weights, columns, shared, 2 * units, out)
        return covariance_part(last_at, weights, columns, last, 2 * units, out)

    own = pack(hidden_states, expert_ids, route_gates)
    gate_weight = load(gate_weight)
    far = send(own, Z2)
    far, up_weight = lax.optimization_barrier((far, up_weight))
    up_weight = load(up_weight)
    blocks = beside(own) + beside(far)
    sizes = [size for size in SIZES if size < 8 * CAP] + [8 * CAP]
    rows, weights, branch = gather(numbers(dp), blocks, sizes)
    parts = project(project_at, rows, gate_weight, up_weight)
    return lax.switch(
        branch[0], [functools.partial(rest, size) for size in sizes], weights, *parts
    )


def solution(mesh):
    placed = (P("dp", "tensor"), P("dp", None), P("dp", None), P("tensor", "dp"), P("tensor", "dp"))
    sizes = (mesh.shape["dp"], mesh.shape["tensor"])
    return jax.shard_map(
        fast if sizes == (8, 4) else any_mesh,
        mesh=mesh,
        in_specs=placed,
        out_specs=P("tensor", "dp"),
        check_vma=False,
    )
```

```python
import functools

import jax
import jax.numpy as jnp
from jax import lax
from jax.experimental import pallas as pl
from jax.experimental.pallas import tpu as pltpu
from jax.sharding import PartitionSpec as P

CAP = 32
LANES = 128
BF, F32 = jnp.bfloat16, jnp.float32
AXES = ("dp", "tensor")
ROWS_OF = (((0,), (0,)), ((), ()))


def pack_rows(token_blocks, weight_blocks):
    member = (weight_blocks > 0).astype(jnp.int32)
    position = jnp.cumsum(member, axis=1) - 1
    slot_index = lax.broadcasted_iota(jnp.int32, (1, CAP, 1), 1)
    picked = (position[:, None, :] == slot_index) & (member[:, None, :] > 0)
    selector = picked.astype(BF)
    packed = jnp.einsum(
        "sct,std->scd", selector, token_blocks, preferred_element_type=F32
    ).astype(BF)
    packed_weight = jnp.einsum(
        "sct,st->sc", selector, weight_blocks, preferred_element_type=F32
    ).astype(BF)
    return (packed.reshape(-1, token_blocks.shape[2]), packed_weight.reshape(-1))


def any_mesh(hidden_states, expert_ids, route_gates, gate_weight, up_weight):
    route_weight = jnp.sum(
        jnp.where(expert_ids == 0, route_gates, jnp.zeros_like(route_gates)), axis=1
    ).astype(BF)
    own_rows, own_weight = pack_rows(hidden_states[None], route_weight[None])
    packed_rows, packed_weight = (
        lax.all_gather(own_rows, "dp", axis=0, tiled=True),
        lax.all_gather(own_weight, "dp", axis=0, tiled=True),
    )
    weight_total = jnp.sum(packed_weight.astype(F32))
    gate_part = jnp.dot(packed_rows, gate_weight, preferred_element_type=F32)
    up_part = jnp.dot(packed_rows, up_weight, preferred_element_type=F32)
    summed = lax.psum_scatter(
        jnp.concatenate([gate_part, up_part], axis=1), "tensor", scatter_dimension=0, tiled=True
    )
    unit_width = gate_weight.shape[1]
    local_keys = (jax.nn.silu(summed[:, :unit_width]) * summed[:, unit_width:]).astype(BF)
    column_keys = lax.all_gather(local_keys, "tensor", axis=0, tiled=True)
    weighted = (packed_weight.astype(F32)[:, None] * column_keys.astype(F32)).astype(BF)
    spread_keys = lax.all_gather(local_keys, "dp", axis=1, tiled=True)
    row_keys = lax.all_to_all(spread_keys, "tensor", split_axis=1, concat_axis=0, tiled=True)
    covariance = lax.dot_general(row_keys, weighted, ROWS_OF, preferred_element_type=F32)
    return covariance / weight_total


def pairs(to):
    number = lambda z, x, y, c: z * 8 + x * 4 + y * 2 + c
    out = []
    for z in range(4):
        for x in range(2):
            for y in range(2):
                for c in range(2):
                    there = to(z, x, y, c)
                    if there is not None:
                        out.append((number(z, x, y, c), number(*there)))
    return out


def inside(z, y):
    return z // 2 == y


CORE = pairs(lambda z, x, y, c: (z, x, y, 1 - c))
Y = pairs(lambda z, x, y, c: (z, x, 1 - y, c))
X = pairs(lambda z, x, y, c: (z, 1 - x, y, c))
Z1 = pairs(lambda z, x, y, c: (z ^ 1, x, y, c))
Z2 = pairs(lambda z, x, y, c: (z ^ 2, x, y, c))
XZ1 = pairs(lambda z, x, y, c: (z ^ 1, 1 - x, y, c))
FAR = pairs(lambda z, x, y, c: (z ^ 2, x, y, c) if inside(z, y) else None)
FAR_Y = pairs(lambda z, x, y, c: (z ^ 2, x, 1 - y, c) if not inside(z, y) else None)
SHARE = pairs(lambda z, x, y, c: (z ^ 1, x, y, c) if c == z % 2 else (z, 1 - x, y, 1 - c))
CROSS = pairs(lambda z, x, y, c: (z ^ 1, 1 - x, y, c) if c == z % 2 else None)

VM = pl.BlockSpec(memory_space=pltpu.VMEM)
SM = pl.BlockSpec(memory_space=pltpu.SMEM)


def send(value, route):
    return lax.ppermute(value, AXES, route)


def cost(flops, nbytes):
    return pl.CostEstimate(flops=flops, bytes_accessed=nbytes, transcendentals=0)


def limit(mebibytes):
    return pltpu.CompilerParams(vmem_limit_bytes=mebibytes << 20)


def shaped(rows, width, kind):
    return jax.ShapeDtypeStruct((rows, width), kind)


def before(rows):
    down = lax.broadcasted_iota(jnp.int32, (rows, rows), 0)
    return jnp.where(down <= lax.broadcasted_iota(jnp.int32, (rows, rows), 1), 1.0, 0.0).astype(BF)


def pack_kernel(ids_ref, gates_ref, tokens_ref, out_ref):
    tokens, width = tokens_ref.shape
    weight = jnp.sum(jnp.where(ids_ref[...] == 0, gates_ref[...], 0.0), axis=0, keepdims=True)
    weight = weight.astype(BF).astype(F32)
    member = jnp.where(weight > 0, 1.0, 0.0)
    position = jnp.dot(
        jnp.broadcast_to(member, (8, tokens)).astype(BF),
        before(tokens),
        preferred_element_type=F32,
    )[:1]
    slot = lax.broadcasted_iota(jnp.int32, (CAP, tokens), 0).astype(F32)
    picked = jnp.where((position - 1.0 == slot) & (member > 0), 1.0, 0.0)
    out_ref[:, :width] = jnp.dot(
        picked.astype(BF), tokens_ref[...], preferred_element_type=F32
    ).astype(BF)
    weights = jnp.sum(picked * weight, axis=1, keepdims=True)
    out_ref[:, width:] = jnp.broadcast_to(weights, (CAP, LANES)).astype(BF)


def pack(hidden_states, expert_ids, route_gates):
    return pl.pallas_call(
        pack_kernel,
        out_shape=shaped(CAP, hidden_states.shape[1] + LANES, BF),
        compiler_params=limit(4),
    )(expert_ids.T, route_gates.T, hidden_states)


def load_kernel(weight_in, weight_ref, sem):
    copy = pltpu.make_async_copy(weight_in, weight_ref, sem)
    copy.start()
    copy.wait()


def load(weight):
    return pl.pallas_call(
        load_kernel,
        in_specs=[pl.BlockSpec(memory_space=pl.ANY)],
        out_specs=VM,
        out_shape=jax.ShapeDtypeStruct(weight.shape, BF),
        scratch_shapes=[pltpu.SemaphoreType.DMA],
        compiler_params=limit(44),
        cost_estimate=cost(0, 2 * weight.size),
    )(weight)


def gather_kernel(sizes, at_ref, *refs):
    blocks, (rows_ref, weights_ref, branch_ref, all_ref) = refs[:8], refs[8:]
    total, depth = rows_ref.shape
    for k, block in enumerate(blocks):
        start = pl.multiple_of((at_ref[0] ^ k) * CAP, CAP)
        all_ref[pl.ds(start, CAP), :] = block[...]
    weights = all_ref[:, depth:]
    member = jnp.where(weights.astype(F32) > 0, 1.0, 0.0)
    count = jnp.sum(member[:, :1])
    branch_ref[0] = sum((count > size).astype(jnp.int32) for size in sizes[:-1])
    member = member.astype(BF)
    position = lax.dot_general(member, before(total), ROWS_OF, preferred_element_type=F32)[:1]
    down = lax.broadcasted_iota(jnp.int32, (total, total), 0)
    across = lax.broadcasted_iota(jnp.int32, (total, total), 1)
    same = jnp.where(down == across, 1.0, 0.0).astype(BF)
    member = lax.dot_general(member, same, ROWS_OF, preferred_element_type=F32)[:1]
    picked = (position - 1.0 == down.astype(F32)) & (member > 0)
    picked = jnp.where(picked, 1.0, 0.0).astype(BF)
    rows_ref[...] = jnp.dot(picked, all_ref[:, :depth], preferred_element_type=F32).astype(BF)
    weights_ref[...] = jnp.dot(picked, weights, preferred_element_type=F32).astype(BF)


def gather(at, blocks, sizes):
    rows, width = 8 * CAP, blocks[0].shape[1]
    return pl.pallas_call(
        functools.partial(gather_kernel, sizes),
        in_specs=[SM] + [VM] * 8,
        out_specs=[VM, VM, SM],
        out_shape=[
            shaped(rows, width - LANES, BF),
            shaped(rows, LANES, BF),
            jax.ShapeDtypeStruct((1,), jnp.int32),
        ],
        scratch_shapes=[pltpu.VMEM((rows, width), BF)],
        compiler_params=limit(6),
        cost_estimate=cost(1 << 28, 1 << 20),
    )(at, *blocks)


def project_kernel(at_ref, rows_ref, gate_ref, up_ref, *outs):
    rows = rows_ref[...]
    quarter = outs[0].shape[1] // 2
    for i, out_ref in enumerate(outs):
        units = pl.ds(pl.multiple_of(at_ref[i] * quarter, quarter), quarter)
        out_ref[:, :quarter] = jnp.dot(rows, gate_ref[:, units], preferred_element_type=F32)
        out_ref[:, quarter:] = jnp.dot(rows, up_ref[:, units], preferred_element_type=F32)


def project(at, rows, gate_weight, up_weight):
    units = gate_weight.shape[1]
    return pl.pallas_call(
        project_kernel,
        in_specs=[SM, VM, VM, VM],
        out_specs=[VM] * 4,
        out_shape=[shaped(rows.shape[0], units // 2, F32)] * 4,
        compiler_params=limit(4),
        cost_estimate=cost(4 * rows.size * units, 1 << 20),
    )(at, rows, gate_weight, up_weight)


def sum_kernel(kept_ref, got_ref, out_ref):
    out_ref[...] = (kept_ref[: out_ref.shape[0]] + got_ref[...]).astype(BF)


def add_up(kept, got):
    return pl.pallas_call(
        sum_kernel,
        in_specs=[VM, VM],
        out_specs=VM,
        out_shape=jax.ShapeDtypeStruct(got.shape, BF),
        compiler_params=limit(4),
        cost_estimate=cost(1 << 18, 1 << 20),
    )(kept, got)


def keys_kernel(kept_ref, got_ref, across_ref, out_ref):
    rows, width = out_ref.shape
    total = kept_ref[:rows] + got_ref[...] + across_ref[...].astype(F32)
    gate = total[:, :width]
    out_ref[...] = (gate / (1.0 + jnp.exp(-gate)) * total[:, width:]).astype(BF)


def keys_of(kept, got, across):
    rows, width = across.shape
    return pl.pallas_call(
        keys_kernel,
        in_specs=[VM, VM, VM],
        out_specs=VM,
        out_shape=shaped(rows, width // 2, BF),
        compiler_params=limit(6),
        cost_estimate=cost(1 << 18, 1 << 20),
    )(kept, got, across)


def assemble_kernel(at_ref, weights_ref, *refs):
    near, far, (columns_ref, panel_ref) = refs[:4], refs[4:8], refs[8:]
    rows, width = near[0].shape
    weights = weights_ref[:rows, :1].astype(F32)
    y, core, is_inside = at_ref[0], at_ref[1], at_ref[2] == 1
    for k in range(4):
        number = (y ^ (k % 2)) * 2 + (core ^ (k // 2))
        units = pl.ds(pl.multiple_of(number * width, width), width)
        keys = near[k][...]
        columns_ref[:, units] = (weights * keys.astype(F32)).astype(BF)
        panel_ref[:, units] = jnp.where(is_inside, keys, far[k][...])


def assemble(at, weights, near, far):
    rows, width = near[0].shape
    shape = shaped(rows, 4 * width, BF)
    return pl.pallas_call(
        assemble_kernel,
        in_specs=[SM] + [VM] * 9,
        out_specs=[VM, VM],
        out_shape=[shape, shape],
        compiler_params=limit(6),
        cost_estimate=cost(1 << 18, 1 << 20),
    )(at, weights, *near, *far)


SIZES = (144, 160, 176, 192, 208)
TILE = 256
BUFFERS = 4


def covariance_kernel(at_ref, weights_ref, columns_ref, panel_ref, *refs):
    out_ref, buffer_ref, sems = refs[-3:]
    units = panel_ref.shape[1]
    steps = units // TILE

    def copy(i):
        start = pl.multiple_of((at_ref[0] + i) * TILE, TILE)
        slot = lax.rem(i, BUFFERS)
        return pltpu.make_async_copy(
            buffer_ref.at[slot], out_ref.at[pl.ds(start, TILE)], sems.at[slot]
        )

    @pl.when(at_ref[1] == 1)
    def _():
        total = jnp.sum(weights_ref[:, :1].astype(F32), axis=0, keepdims=True)
        scale = 1.0 / total

        def step(i, carry):
            @pl.when(i >= BUFFERS)
            def _():
                copy(i - BUFFERS).wait()

            part = panel_ref[:, pl.ds(pl.multiple_of(i * TILE, TILE), TILE)]
            value = lax.dot_general(part, columns_ref[...], ROWS_OF, preferred_element_type=F32)
            buffer_ref[lax.rem(i, BUFFERS)] = value * scale
            copy(i).start()
            return carry

        lax.fori_loop(0, steps, step, 0)

        def finish(i, carry):
            copy(i).wait()
            return carry

        lax.fori_loop(steps - BUFFERS, steps, finish, 0)


def covariance_part(at, weights, columns, panel, out_rows, into):
    rows, units = panel.shape
    width = columns.shape[1]
    args = [at, weights, columns, panel]
    in_specs = [SM, VM, VM, VM]
    aliases = {}
    if into is not None:
        args.append(into)
        in_specs.append(pl.BlockSpec(memory_space=pl.ANY))
        aliases = {4: 0}
    return pl.pallas_call(
        covariance_kernel,
        in_specs=in_specs,
        out_specs=pl.BlockSpec(memory_space=pl.ANY),
        out_shape=shaped(out_rows, width, F32),
        scratch_shapes=[
            pltpu.VMEM((BUFFERS, TILE, width), F32),
            pltpu.SemaphoreType.DMA((BUFFERS,)),
        ],
        input_output_aliases=aliases,
        compiler_params=limit(14),
        cost_estimate=cost(2 * rows * units * width, 4 * units * width),
    )(*args)


def numbers(*values):
    return jnp.stack([jnp.asarray(v, jnp.int32) for v in values])


def fast(hidden_states, expert_ids, route_gates, gate_weight, up_weight):
    units = gate_weight.shape[1]
    dp, tensor = lax.axis_index("dp"), lax.axis_index("tensor")
    z, x, y, core = dp // 2, dp % 2, tensor // 2, tensor % 2
    is_home, is_inside = core == z % 2, y == z // 2
    quarters = [(1 - y, 1 - core), (y, 1 - core), (1 - y, core), (y, core)]
    project_at = numbers(*[of_y * 2 + of_core for of_y, of_core in quarters])
    tiles = units // 2 // TILE
    mine_at = numbers(2 * tiles * x, is_home)
    shared_at = 2 * tiles * jnp.where(is_home, 1 - x, x)
    shared_at = [numbers(shared_at + k * tiles, 1) for k in range(2)]
    last_at = [numbers(2 * tiles * (1 - x) + k * tiles, core != z % 2) for k in range(2)]
    keys_at = numbers(y, core, is_inside)

    def beside(mine):
        return [mine, send(mine, X), send(mine, Z1), send(mine, XZ1)]

    def rest(rows, weights, given_across, given, kept_across, kept):
        across = add_up(kept_across, send(given_across[:rows], CORE))
        arrived = send(across, Y)
        keys = keys_of(kept, send(given[:rows], CORE), arrived)
        far = [send(keys, FAR)]
        swapped = send(keys, CORE)
        keys, swapped = lax.optimization_barrier((keys, swapped))
        far.append(send(keys, FAR_Y))
        near = [keys, send(keys, Y)]
        near += [swapped, send(near[1], CORE)]
        far += [send(k, CORE) for k in far]
        columns, panel = assemble(keys_at, weights, near, far)
        shared = [send(half, SHARE) for half in jnp.split(panel, 2, axis=1)]
        panel, _ = lax.optimization_barrier((panel, send(panel[:16, :LANES], CORE)))
        crossed = [send(half, CROSS) for half in jnp.split(panel, 2, axis=1)]
        out = covariance_part(mine_at, weights, columns, panel, 2 * units, None)
        for places, halves in ((shared_at, shared), (last_at, crossed)):
            for at, half in zip(places, halves):
                out = covariance_part(at, weights, columns, half, 2 * units, out)
        return out

    own = pack(hidden_states, expert_ids, route_gates)
    gate_weight = load(gate_weight)
    far = send(own, Z2)
    far, up_weight = lax.optimization_barrier((far, up_weight))
    up_weight = load(up_weight)
    blocks = beside(own) + beside(far)
    sizes = [size for size in SIZES if size < 8 * CAP] + [8 * CAP]
    rows, weights, branch = gather(numbers(dp), blocks, sizes)
    parts = project(project_at, rows, gate_weight, up_weight)
    return lax.switch(
        branch[0], [functools.partial(rest, size) for size in sizes], weights, *parts
    )


def solution(mesh):
    placed = (P("dp", "tensor"), P("dp", None), P("dp", None), P("tensor", "dp"), P("tensor", "dp"))
    sizes = (mesh.shape["dp"], mesh.shape["tensor"])
    return jax.shard_map(
        fast if sizes == (8, 4) else any_mesh,
        mesh=mesh,
        in_specs=placed,
        out_specs=P("tensor", "dp"),
        check_vma=False,
    )
```

```python
import functools

import jax
import jax.numpy as jnp
from jax import lax
from jax.experimental import pallas as pl
from jax.experimental.pallas import tpu as pltpu
from jax.sharding import PartitionSpec as P

CAP = 32
LANES = 128
BF, F32 = jnp.bfloat16, jnp.float32
AXES = ("dp", "tensor")
ROWS_OF = (((0,), (0,)), ((), ()))


def pack_rows(token_blocks, weight_blocks):
    member = (weight_blocks > 0).astype(jnp.int32)
    position = jnp.cumsum(member, axis=1) - 1
    slot_index = lax.broadcasted_iota(jnp.int32, (1, CAP, 1), 1)
    picked = (position[:, None, :] == slot_index) & (member[:, None, :] > 0)
    selector = picked.astype(BF)
    packed = jnp.einsum(
        "sct,std->scd", selector, token_blocks, preferred_element_type=F32
    ).astype(BF)
    packed_weight = jnp.einsum(
        "sct,st->sc", selector, weight_blocks, preferred_element_type=F32
    ).astype(BF)
    return (packed.reshape(-1, token_blocks.shape[2]), packed_weight.reshape(-1))


def any_mesh(hidden_states, expert_ids, route_gates, gate_weight, up_weight):
    route_weight = jnp.sum(
        jnp.where(expert_ids == 0, route_gates, jnp.zeros_like(route_gates)), axis=1
    ).astype(BF)
    own_rows, own_weight = pack_rows(hidden_states[None], route_weight[None])
    packed_rows, packed_weight = (
        lax.all_gather(own_rows, "dp", axis=0, tiled=True),
        lax.all_gather(own_weight, "dp", axis=0, tiled=True),
    )
    weight_total = jnp.sum(packed_weight.astype(F32))
    gate_part = jnp.dot(packed_rows, gate_weight, preferred_element_type=F32)
    up_part = jnp.dot(packed_rows, up_weight, preferred_element_type=F32)
    summed = lax.psum_scatter(
        jnp.concatenate([gate_part, up_part], axis=1), "tensor", scatter_dimension=0, tiled=True
    )
    unit_width = gate_weight.shape[1]
    local_keys = (jax.nn.silu(summed[:, :unit_width]) * summed[:, unit_width:]).astype(BF)
    column_keys = lax.all_gather(local_keys, "tensor", axis=0, tiled=True)
    weighted = (packed_weight.astype(F32)[:, None] * column_keys.astype(F32)).astype(BF)
    spread_keys = lax.all_gather(local_keys, "dp", axis=1, tiled=True)
    row_keys = lax.all_to_all(spread_keys, "tensor", split_axis=1, concat_axis=0, tiled=True)
    covariance = lax.dot_general(row_keys, weighted, ROWS_OF, preferred_element_type=F32)
    return covariance / weight_total


def pairs(to):
    number = lambda z, x, y, c: z * 8 + x * 4 + y * 2 + c
    out = []
    for z in range(4):
        for x in range(2):
            for y in range(2):
                for c in range(2):
                    there = to(z, x, y, c)
                    if there is not None:
                        out.append((number(z, x, y, c), number(*there)))
    return out


def inside(z, y):
    return z // 2 == y


CORE = pairs(lambda z, x, y, c: (z, x, y, 1 - c))
Y = pairs(lambda z, x, y, c: (z, x, 1 - y, c))
X = pairs(lambda z, x, y, c: (z, 1 - x, y, c))
Z1 = pairs(lambda z, x, y, c: (z ^ 1, x, y, c))
Z2 = pairs(lambda z, x, y, c: (z ^ 2, x, y, c))
XZ1 = pairs(lambda z, x, y, c: (z ^ 1, 1 - x, y, c))
FAR = pairs(lambda z, x, y, c: (z ^ 2, x, y, c) if inside(z, y) else None)
FAR_Y = pairs(lambda z, x, y, c: (z ^ 2, x, 1 - y, c) if not inside(z, y) else None)
SHARE = pairs(lambda z, x, y, c: (z ^ 1, x, y, c) if c == z % 2 else (z, 1 - x, y, 1 - c))
CROSS = pairs(lambda z, x, y, c: (z ^ 1, 1 - x, y, c) if c == z % 2 else None)

VM = pl.BlockSpec(memory_space=pltpu.VMEM)
SM = pl.BlockSpec(memory_space=pltpu.SMEM)


def send(value, route):
    return lax.ppermute(value, AXES, route)


def cost(flops, nbytes):
    return pl.CostEstimate(flops=flops, bytes_accessed=nbytes, transcendentals=0)


def limit(mebibytes):
    return pltpu.CompilerParams(vmem_limit_bytes=mebibytes << 20)


def shaped(rows, width, kind):
    return jax.ShapeDtypeStruct((rows, width), kind)


def before(rows):
    down = lax.broadcasted_iota(jnp.int32, (rows, rows), 0)
    return jnp.where(down <= lax.broadcasted_iota(jnp.int32, (rows, rows), 1), 1.0, 0.0).astype(BF)


def pack_kernel(weight_ref, tokens_ref, out_ref):
    tokens, width = tokens_ref.shape
    weight = weight_ref[...].astype(BF).astype(F32)
    member = jnp.where(weight > 0, 1.0, 0.0)
    position = jnp.dot(
        jnp.broadcast_to(member, (8, tokens)).astype(BF),
        before(tokens),
        preferred_element_type=F32,
    )[:1]
    slot = lax.broadcasted_iota(jnp.int32, (CAP, tokens), 0).astype(F32)
    picked = jnp.where((position - 1.0 == slot) & (member > 0), 1.0, 0.0)
    out_ref[:, :width] = jnp.dot(
        picked.astype(BF), tokens_ref[...], preferred_element_type=F32
    ).astype(BF)
    weights = jnp.sum(picked * weight, axis=1, keepdims=True)
    out_ref[:, width:] = jnp.broadcast_to(weights, (CAP, LANES)).astype(BF)


def pack(hidden_states, expert_ids, route_gates):
    weight = jnp.sum(jnp.where(expert_ids == 0, route_gates, 0.0), axis=1)
    return pl.pallas_call(
        pack_kernel,
        out_shape=shaped(CAP, hidden_states.shape[1] + LANES, BF),
        compiler_params=limit(4),
    )(weight[None, :], hidden_states)


def load_kernel(weight_in, weight_ref, sem):
    copy = pltpu.make_async_copy(weight_in, weight_ref, sem)
    copy.start()
    copy.wait()


def load(weight):
    return pl.pallas_call(
        load_kernel,
        in_specs=[pl.BlockSpec(memory_space=pl.ANY)],
        out_specs=VM,
        out_shape=jax.ShapeDtypeStruct(weight.shape, BF),
        scratch_shapes=[pltpu.SemaphoreType.DMA],
        compiler_params=limit(44),
        cost_estimate=cost(0, 2 * weight.size),
    )(weight)


def gather_kernel(sizes, at_ref, *refs):
    blocks, (rows_ref, weights_ref, branch_ref, all_ref) = refs[:8], refs[8:]
    total, depth = rows_ref.shape
    for k, block in enumerate(blocks):
        start = pl.multiple_of((at_ref[0] ^ k) * CAP, CAP)
        all_ref[pl.ds(start, CAP), :] = block[...]
    weights = all_ref[:, depth:]
    member = jnp.where(weights.astype(F32) > 0, 1.0, 0.0)
    count = jnp.sum(member[:, :1])
    branch_ref[0] = sum((count > size).astype(jnp.int32) for size in sizes[:-1])
    member = member.astype(BF)
    position = lax.dot_general(member, before(total), ROWS_OF, preferred_element_type=F32)[:1]
    down = lax.broadcasted_iota(jnp.int32, (total, total), 0)
    across = lax.broadcasted_iota(jnp.int32, (total, total), 1)
    same = jnp.where(down == across, 1.0, 0.0).astype(BF)
    member = lax.dot_general(member, same, ROWS_OF, preferred_element_type=F32)[:1]
    picked = (position - 1.0 == down.astype(F32)) & (member > 0)
    picked = jnp.where(picked, 1.0, 0.0).astype(BF)
    rows_ref[...] = jnp.dot(picked, all_ref[:, :depth], preferred_element_type=F32).astype(BF)
    weights_ref[...] = jnp.dot(picked, weights, preferred_element_type=F32).astype(BF)


def gather(at, blocks, sizes):
    rows, width = 8 * CAP, blocks[0].shape[1]
    return pl.pallas_call(
        functools.partial(gather_kernel, sizes),
        in_specs=[SM] + [VM] * 8,
        out_specs=[VM, VM, SM],
        out_shape=[
            shaped(rows, width - LANES, BF),
            shaped(rows, LANES, BF),
            jax.ShapeDtypeStruct((1,), jnp.int32),
        ],
        scratch_shapes=[pltpu.VMEM((rows, width), BF)],
        compiler_params=limit(6),
        cost_estimate=cost(1 << 28, 1 << 20),
    )(at, *blocks)


def project_kernel(at_ref, rows_ref, gate_ref, up_ref, *outs):
    rows = rows_ref[...]
    quarter = outs[0].shape[1] // 2
    for i, out_ref in enumerate(outs):
        units = pl.ds(pl.multiple_of(at_ref[i] * quarter, quarter), quarter)
        out_ref[:, :quarter] = jnp.dot(rows, gate_ref[:, units], preferred_element_type=F32)
        out_ref[:, quarter:] = jnp.dot(rows, up_ref[:, units], preferred_element_type=F32)


def project(at, rows, gate_weight, up_weight):
    units = gate_weight.shape[1]
    return pl.pallas_call(
        project_kernel,
        in_specs=[SM, VM, VM, VM],
        out_specs=[VM] * 4,
        out_shape=[shaped(rows.shape[0], units // 2, F32)] * 4,
        compiler_params=limit(4),
        cost_estimate=cost(4 * rows.size * units, 1 << 20),
    )(at, rows, gate_weight, up_weight)


def sum_kernel(kept_ref, got_ref, out_ref):
    out_ref[...] = (kept_ref[: out_ref.shape[0]] + got_ref[...]).astype(BF)


def add_up(kept, got):
    return pl.pallas_call(
        sum_kernel,
        in_specs=[VM, VM],
        out_specs=VM,
        out_shape=jax.ShapeDtypeStruct(got.shape, BF),
        compiler_params=limit(4),
        cost_estimate=cost(1 << 18, 1 << 20),
    )(kept, got)


def keys_kernel(kept_ref, got_ref, across_ref, out_ref):
    rows, width = out_ref.shape
    total = kept_ref[:rows] + got_ref[...] + across_ref[...].astype(F32)
    gate = total[:, :width]
    out_ref[...] = (gate / (1.0 + jnp.exp(-gate)) * total[:, width:]).astype(BF)


def keys_of(kept, got, across):
    rows, width = across.shape
    return pl.pallas_call(
        keys_kernel,
        in_specs=[VM, VM, VM],
        out_specs=VM,
        out_shape=shaped(rows, width // 2, BF),
        compiler_params=limit(6),
        cost_estimate=cost(1 << 18, 1 << 20),
    )(kept, got, across)


def assemble_kernel(at_ref, weights_ref, *refs):
    near, far, (columns_ref, panel_ref) = refs[:4], refs[4:8], refs[8:]
    rows, width = near[0].shape
    weights = weights_ref[:rows, :1].astype(F32)
    y, core, is_inside = at_ref[0], at_ref[1], at_ref[2] == 1
    for k in range(4):
        number = (y ^ (k % 2)) * 2 + (core ^ (k // 2))
        units = pl.ds(pl.multiple_of(number * width, width), width)
        keys = near[k][...]
        columns_ref[:, units] = (weights * keys.astype(F32)).astype(BF)
        panel_ref[:, units] = jnp.where(is_inside, keys, far[k][...])


def assemble(at, weights, near, far):
    rows, width = near[0].shape
    shape = shaped(rows, 4 * width, BF)
    return pl.pallas_call(
        assemble_kernel,
        in_specs=[SM] + [VM] * 9,
        out_specs=[VM, VM],
        out_shape=[shape, shape],
        compiler_params=limit(6),
        cost_estimate=cost(1 << 18, 1 << 20),
    )(at, weights, *near, *far)


SIZES = (144, 160, 176, 192, 208)
TILE = 256
BUFFERS = 4


def covariance_kernel(at_ref, weights_ref, columns_ref, panel_ref, *refs):
    out_ref, buffer_ref, sems = refs[-3:]
    units = panel_ref.shape[1]
    steps = units // TILE

    def copy(i):
        start = pl.multiple_of((at_ref[0] + i) * TILE, TILE)
        slot = lax.rem(i, BUFFERS)
        return pltpu.make_async_copy(
            buffer_ref.at[slot], out_ref.at[pl.ds(start, TILE)], sems.at[slot]
        )

    @pl.when(at_ref[1] == 1)
    def _():
        total = jnp.sum(weights_ref[:, :1].astype(F32), axis=0, keepdims=True)
        scale = 1.0 / total

        def step(i, carry):
            @pl.when(i >= BUFFERS)
            def _():
                copy(i - BUFFERS).wait()

            part = panel_ref[:, pl.ds(pl.multiple_of(i * TILE, TILE), TILE)]
            value = lax.dot_general(part, columns_ref[...], ROWS_OF, preferred_element_type=F32)
            buffer_ref[lax.rem(i, BUFFERS)] = value * scale
            copy(i).start()
            return carry

        lax.fori_loop(0, steps, step, 0)

        def finish(i, carry):
            copy(i).wait()
            return carry

        lax.fori_loop(steps - BUFFERS, steps, finish, 0)


def covariance_part(at, weights, columns, panel, out_rows, into):
    rows, units = panel.shape
    width = columns.shape[1]
    args = [at, weights, columns, panel]
    in_specs = [SM, VM, VM, VM]
    aliases = {}
    if into is not None:
        args.append(into)
        in_specs.append(pl.BlockSpec(memory_space=pl.ANY))
        aliases = {4: 0}
    return pl.pallas_call(
        covariance_kernel,
        in_specs=in_specs,
        out_specs=pl.BlockSpec(memory_space=pl.ANY),
        out_shape=shaped(out_rows, width, F32),
        scratch_shapes=[
            pltpu.VMEM((BUFFERS, TILE, width), F32),
            pltpu.SemaphoreType.DMA((BUFFERS,)),
        ],
        input_output_aliases=aliases,
        compiler_params=limit(14),
        cost_estimate=cost(2 * rows * units * width, 4 * units * width),
    )(*args)


def numbers(*values):
    return jnp.stack([jnp.asarray(v, jnp.int32) for v in values])


def fast(hidden_states, expert_ids, route_gates, gate_weight, up_weight):
    units = gate_weight.shape[1]
    dp, tensor = lax.axis_index("dp"), lax.axis_index("tensor")
    z, x, y, core = dp // 2, dp % 2, tensor // 2, tensor % 2
    is_home, is_inside = core == z % 2, y == z // 2
    quarters = [(1 - y, 1 - core), (y, 1 - core), (1 - y, core), (y, core)]
    project_at = numbers(*[of_y * 2 + of_core for of_y, of_core in quarters])
    tiles = units // 2 // TILE
    mine_at = numbers(2 * tiles * x, is_home)
    shared_at = 2 * tiles * jnp.where(is_home, 1 - x, x)
    shared_at = [numbers(shared_at + k * tiles, 1) for k in range(2)]
    last_at = [numbers(2 * tiles * (1 - x) + k * tiles, core != z % 2) for k in range(2)]
    keys_at = numbers(y, core, is_inside)

    def beside(mine):
        return [mine, send(mine, X), send(mine, Z1), send(mine, XZ1)]

    def rest(rows, weights, given_across, given, kept_across, kept):
        across = add_up(kept_across, send(given_across[:rows], CORE))
        arrived = send(across, Y)
        keys = keys_of(kept, send(given[:rows], CORE), arrived)
        far = [send(keys, FAR)]
        swapped = send(keys, CORE)
        keys, swapped = lax.optimization_barrier((keys, swapped))
        far.append(send(keys, FAR_Y))
        near = [keys, send(keys, Y)]
        near += [swapped, send(near[1], CORE)]
        far += [send(k, CORE) for k in far]
        columns, panel = assemble(keys_at, weights, near, far)
        shared = [send(half, SHARE) for half in jnp.split(panel, 2, axis=1)]
        panel, _ = lax.optimization_barrier((panel, send(panel[:16, :LANES], CORE)))
        crossed = [send(half, CROSS) for half in jnp.split(panel, 2, axis=1)]
        out = covariance_part(mine_at, weights, columns, panel, 2 * units, None)
        for places, halves in ((shared_at, shared), (last_at, crossed)):
            for at, half in zip(places, halves):
                out = covariance_part(at, weights, columns, half, 2 * units, out)
        return out

    own = pack(hidden_states, expert_ids, route_gates)
    gate_weight = load(gate_weight)
    far = send(own, Z2)
    far, up_weight = lax.optimization_barrier((far, up_weight))
    up_weight = load(up_weight)
    blocks = beside(own) + beside(far)
    sizes = [size for size in SIZES if size < 8 * CAP] + [8 * CAP]
    rows, weights, branch = gather(numbers(dp), blocks, sizes)
    parts = project(project_at, rows, gate_weight, up_weight)
    return lax.switch(
        branch[0], [functools.partial(rest, size) for size in sizes], weights, *parts
    )


def solution(mesh):
    placed = (P("dp", "tensor"), P("dp", None), P("dp", None), P("tensor", "dp"), P("tensor", "dp"))
    sizes = (mesh.shape["dp"], mesh.shape["tensor"])
    return jax.shard_map(
        fast if sizes == (8, 4) else any_mesh,
        mesh=mesh,
        in_specs=placed,
        out_specs=P("tensor", "dp"),
        check_vma=False,
    )
```
